512 devices in a mesh: section: 32 (over x, z_lo, core), aux: 2 (over z_hi), dp: 8 (over y).
Axes of the slice: x: 4, y: 8, z: 8 (z_hi: 2, z_lo: 4; z = z_hi * 4 + z_lo), core: 2. Of those that a mesh axis runs over, the one named last changes fastest.
Arguments:
- aux_rows: bfloat16 [32, 8, 256, 2048], P(None, 'dp', 'section', 'aux'), may hold values from -30 to 30
- predictors: bfloat16 [2, 32, 32, 8, 8, 512], P('aux', None, 'section', 'dp'), may hold values from -0.125 to 0.125
- queries: bfloat16 [32, 2048, 4096], P('section', 'dp', 'aux'), may hold values from -600 to 600
- target: bfloat16 [32, 2048, 4096], P('section', 'dp', 'aux'), may hold values from -3 to 3
- lengths: int32 [8, 4], P('dp'), may hold values from 1 to 128, 256 in all within a row
Outputs:
- grad_rows: bfloat16 [32, 8, 256, 2048], P(None, 'dp', 'section', 'aux')
- grad_predictors: float32 [2, 32, 32, 8, 8, 512], P('aux', None, 'section', 'dp')
The draws below stay inside these ranges and needn't reach their ends.
Inputs may be any that keep to these rules, and one draw needn't show every extreme that they name: Each row holds 4 prompt lengths summing to 256; the largest is exactly 128.
All inputs are finite; a program needn't handle non-finite values.
Results may differ from the reference program's by a relative error of at most 0.024.
The reference program's roundings to bfloat16 on the way count: a program that leaves them out, or rounds other values in their place, can miss the bound.
Values may be sent and summed in bfloat16 or wider, within the bound.
No kernel may reach another device: no remote copies, remote signals or barrier semaphores. Data moves between devices by JAX's collectives and lax.ppermute only.
A program may use at most 64 MiB of HBM per device.

```python
import math
import jax
import jax.numpy as jnp
import numpy as np
from jax import lax

D_AUX = 2048
KV_HEADS = 4
QHEADS = 32
HEAD_DIM = 128
DOCS = 4
TOK_DEV = 256
MOST_DOC = 128
LAYERS = 32
KVW = 512
ROWS_BLK = 8
TOKENS = 2048
N_SECTION = 32
N_DP = 8


def draw_aux_rows(key, part):
    key = jax.random.fold_in(key, 11)
    shape = (LAYERS, N_DP, TOK_DEV, D_AUX)
    base = jax.random.normal(key, shape, jnp.float32)
    return jnp.clip(base, -30.0, 30.0).astype(jnp.bfloat16)


def draw_queries(key, part):
    key = jax.random.fold_in(key, 23)
    shape = (LAYERS, TOKENS, QHEADS * HEAD_DIM)
    base = jnp.clip(jax.random.normal(key, shape, jnp.float32), -6.0, 6.0)
    return base.astype(jnp.bfloat16)


def shard_levels(key, dims, shards, smallest, high):
    gain, own = 1.0, jax.random.fold_in(key, 6)
    for axis_at, parts in shards:
        draws = jnp.exp(jax.random.uniform(jax.random.fold_in(own, axis_at), (parts,), jnp.float32, smallest / len(shards), high / len(shards)))
        gain = gain * jnp.repeat(draws, dims[axis_at] // parts).reshape([-1 if axis == axis_at else 1 for axis in range(len(dims))])
    return gain


def length_profile(amount, total, limit, skew):
    weights = [(1 << 20) // math.isqrt(grade ** skew) + 1 for grade in range(2, amount + 1)]
    spare, holding = total - limit - (amount - 1), [1] * (amount - 1)
    while spare > 0:
        free = [i for i in range(amount - 1) if holding[i] < limit]
        mass, left = sum([weights[i] for i in free]), spare
        for i in free:
            addition = min(limit - holding[i], max(1, left * weights[i] // mass), spare)
            holding[i] = holding[i] + addition
            spare = spare - addition
    return np.array([limit] + holding)


def ragged(stream_key, count, total, most, slope):
    if count == 2:
        one = jax.random.randint(stream_key, (), max(1, total - most), min(most, total - 1) + 1)
        return jnp.stack([one, total - one])
    sizes = jnp.asarray(length_profile(count, total, most, slope), jnp.int32)
    couples = (count - 1) // 2
    donor, receiver = sizes[1:1 + 2 * couples:2], sizes[2:2 + 2 * couples:2]
    slack = jnp.minimum(donor - 1, most - receiver)
    moved = jax.random.randint(jax.random.fold_in(stream_key, 1), (couples,), 0, 1 << 20) % (slack + 1)
    sizes = sizes.at[1:1 + 2 * couples:2].set(donor - moved).at[2:2 + 2 * couples:2].set(receiver + moved)
    return sizes[jax.random.permutation(jax.random.fold_in(stream_key, 2), count)]


def centred(key, extent, scale, reach, cuts=(), held_as=jnp.bfloat16):
    values = jax.random.normal(key, extent, jnp.float32) * scale
    if len(cuts) > 0:
        values = shard_levels(key, extent, cuts, -0.22, 0.18) * values
    return jnp.clip(values, min=-reach, max=reach).astype(held_as)


def setup_inputs(seed: int = 0) -> dict:
    arg_keys = jax.random.split(jax.random.key(seed), 6)
    aux_rows = draw_aux_rows(jax.random.fold_in(arg_keys[5], 71), 0)
    predictors = centred(arg_keys[1], (2, LAYERS, N_SECTION, N_DP, ROWS_BLK, KVW), D_AUX ** -0.5, 0.125, ((0, 2), (2, 32), (3, 8)))
    queries = draw_queries(jax.random.fold_in(arg_keys[5], 71), 0)
    target = centred(arg_keys[3], (LAYERS, TOKENS, QHEADS * HEAD_DIM), 0.5, 3.0, ((0, 32), (1, 8), (2, 2)))
    lengths = jax.vmap(lambda own: ragged(own, DOCS, TOK_DEV, MOST_DOC, 2))(jax.random.split(arg_keys[4], N_DP)).reshape((N_DP, DOCS)).astype(jnp.int32)
    return dict(aux_rows=aux_rows, predictors=predictors, queries=queries, target=target, lengths=lengths)


def doc_mask(lens, count):
    ends = jnp.cumsum(lens.astype(jnp.int32))
    pos = jnp.arange(count, dtype=jnp.int32)
    docs = lax.optimization_barrier(jnp.sum((pos[:, None] >= ends[None, :]).astype(jnp.int32), axis=1))
    return (docs[:, None] == docs[None, :]) & (pos[None, :] <= pos[:, None])

def attend_grads(qrows, keys, values, goal, mask):
    tok, kvh, hdim = keys.shape
    group = qrows.shape[1] // (kvh * hdim)
    scale = 1.0 / math.sqrt(hdim)
    q_four = qrows.astype(jnp.float32).reshape(tok, kvh, group, hdim)
    key_f = keys.astype(jnp.float32)
    val_f = values.astype(jnp.float32)
    scores = jnp.einsum('ihgd,jhd->hgij', q_four, key_f) * scale
    scores = jnp.where(mask[None, None], scores, -1e+30)
    top = lax.optimization_barrier(jnp.max(scores, axis=-1, keepdims=True))
    expo = jnp.exp(scores - top)
    probs = expo / lax.optimization_barrier(jnp.sum(expo, axis=-1, keepdims=True))
    probs_b = probs.astype(jnp.bfloat16).astype(jnp.float32)
    attn_out = jnp.einsum('hgij,jhd->ihgd', probs_b, val_f).reshape(tok, -1)
    dout = attn_out - goal.astype(jnp.float32)
    dout_b = dout.astype(jnp.bfloat16).astype(jnp.float32).reshape(tok, kvh, group, hdim)
    dprob = jnp.einsum('ihgd,jhd->hgij', dout_b, val_f)
    delta = lax.optimization_barrier(jnp.sum((dout * attn_out).reshape(tok, kvh, group, hdim), axis=-1))
    delta = jnp.transpose(delta, (1, 2, 0))[..., None]
    dscore = (probs * (dprob - delta) * scale).astype(jnp.bfloat16).astype(jnp.float32)
    dkeys = jnp.einsum('hgij,ihgd->jhd', dscore, q_four)
    dvalues = jnp.einsum('hgij,ihgd->jhd', probs_b, dout_b)
    return (dkeys.astype(jnp.bfloat16), dvalues.astype(jnp.bfloat16))

def settle(values):
    return lax.optimization_barrier(values.astype(jnp.bfloat16)).astype(jnp.float32)

def reference(aux_rows, predictors, queries, target, lengths):
    width = KV_HEADS * HEAD_DIM

    def one_layer(index):
        rows = aux_rows[index].reshape(TOKENS, D_AUX)
        w_keys = predictors[0, index].reshape(D_AUX, width)
        w_values = predictors[1, index].reshape(D_AUX, width)
        keys = jnp.dot(rows, w_keys, preferred_element_type=jnp.float32).astype(jnp.bfloat16)
        values = jnp.dot(rows, w_values, preferred_element_type=jnp.float32).astype(jnp.bfloat16)
        qrows = queries[index]
        goal = target[index]

        def one_batch(batch):
            start = batch * TOK_DEV

            def cut(array):
                return lax.dynamic_slice_in_dim(array, start, TOK_DEV, 0)
            mask = doc_mask(lengths[batch], TOK_DEV)
            dkeys, dvalues = attend_grads(cut(qrows), cut(keys).reshape(TOK_DEV, KV_HEADS, HEAD_DIM), cut(values).reshape(TOK_DEV, KV_HEADS, HEAD_DIM), cut(goal), mask)
            dkeys = dkeys.reshape(TOK_DEV, width)
            dvalues = dvalues.reshape(TOK_DEV, width)
            block = cut(rows)
            grad_keys = settle(jnp.dot(block.T, dkeys, preferred_element_type=jnp.float32))
            grad_values = settle(jnp.dot(block.T, dvalues, preferred_element_type=jnp.float32))
            from_keys = settle(jnp.dot(dkeys, w_keys.T, preferred_element_type=jnp.float32))
            from_values = settle(jnp.dot(dvalues, w_values.T, preferred_element_type=jnp.float32))
            return (grad_keys, grad_values, (from_keys + from_values).astype(jnp.bfloat16))
        grad_keys, grad_values, row_grads = lax.map(one_batch, jnp.arange(N_DP, dtype=jnp.int32))
        shape = (N_SECTION, N_DP, D_AUX // (N_SECTION * N_DP), width)
        both = jnp.stack([lax.optimization_barrier(jnp.sum(grad_keys, axis=0)).reshape(shape), lax.optimization_barrier(jnp.sum(grad_values, axis=0)).reshape(shape)])
        return (row_grads, both)
    grad_rows, grads = lax.map(one_layer, jnp.arange(N_SECTION, dtype=jnp.int32))
    grad_predictors = jnp.moveaxis(grads, 1, 0)
    return (grad_rows, grad_predictors)
```

```python
import math

import jax
import jax.numpy as jnp
from jax import lax
from jax.sharding import PartitionSpec as P

HEAD_DIM = 128


def doc_mask(lens, count):
    ends = jnp.cumsum(lens)
    pos = jnp.arange(count, dtype=jnp.int32)
    docs = jnp.sum((pos[:, None] >= ends[None, :]).astype(jnp.int32), axis=1)
    return (docs[:, None] == docs[None, :]) & (pos[None, :] <= pos[:, None])


def attend_grads(qrows, keys, values, goal, mask):
    tok, kvh, hdim = keys.shape
    group = qrows.shape[1] // (kvh * hdim)
    scale = 1.0 / math.sqrt(hdim)
    q_four = qrows.reshape(tok, kvh, group, hdim)
    scores = jnp.einsum("ihgd,jhd->hgij", q_four, keys, preferred_element_type=jnp.float32) * scale
    scores = jnp.where(mask[None, None], scores, -1e30)
    top = jnp.max(scores, axis=-1, keepdims=True)
    expo = jnp.exp(scores - top)
    probs = expo / jnp.sum(expo, axis=-1, keepdims=True)
    probs_b = probs.astype(jnp.bfloat16)
    attn_out = jnp.einsum(
        "hgij,jhd->ihgd", probs_b, values, preferred_element_type=jnp.float32
    ).reshape(tok, -1)
    dout = attn_out - goal.astype(jnp.float32)
    dout_b = dout.astype(jnp.bfloat16).reshape(tok, kvh, group, hdim)
    dprob = jnp.einsum("ihgd,jhd->hgij", dout_b, values, preferred_element_type=jnp.float32)
    delta = jnp.sum((dout * attn_out).reshape(tok, kvh, group, hdim), axis=-1)
    delta = jnp.transpose(delta, (1, 2, 0))[..., None]
    dscore = (probs * (dprob - delta) * scale).astype(jnp.bfloat16)
    dkeys = jnp.einsum("hgij,ihgd->jhd", dscore, q_four, preferred_element_type=jnp.float32)
    dvalues = jnp.einsum("hgij,ihgd->jhd", probs_b, dout_b, preferred_element_type=jnp.float32)
    return (dkeys.astype(jnp.bfloat16), dvalues.astype(jnp.bfloat16))


def per_device(aux_rows, predictors, queries, target, lengths):
    sections = lax.axis_size("section")
    auxes = lax.axis_size("aux")
    shards = lax.axis_size("dp")
    both = ("section", "aux")
    peers = sections * auxes
    blk, width = predictors.shape[4:]
    part = width // auxes
    rows_each, feats = aux_rows.shape[2:]
    tok = sections * rows_each

    w_out = predictors.reshape(sections, blk, auxes, part).swapaxes(1, 2).reshape(peers, blk, part)
    w_in = lax.all_to_all(w_out, both, split_axis=0, concat_axis=0, tiled=True)
    w_all = lax.all_gather(w_in, "dp", axis=0)
    weight = jnp.transpose(
        w_all.reshape(shards, sections, auxes, blk, part), (1, 0, 3, 2, 4)
    ).reshape(sections * shards * blk, auxes * part)

    r_out = jnp.broadcast_to(
        aux_rows.reshape(sections, 1, rows_each, feats), (sections, auxes, rows_each, feats)
    ).reshape(peers, rows_each, feats)
    r_in = lax.all_to_all(r_out, both, split_axis=0, concat_axis=0, tiled=True)
    rows = jnp.swapaxes(r_in.reshape(sections, auxes, rows_each, feats), 1, 2).reshape(tok, -1)

    cache = jnp.dot(rows, weight, preferred_element_type=jnp.float32).astype(jnp.bfloat16)
    keys = cache[:, :part].reshape(tok, part // HEAD_DIM, HEAD_DIM)
    values = cache[:, part:].reshape(tok, part // HEAD_DIM, HEAD_DIM)
    mask = doc_mask(lengths[0], tok)
    dkeys, dvalues = attend_grads(queries[0], keys, values, target[0], mask)
    dcache = jnp.concatenate([dkeys.reshape(tok, part), dvalues.reshape(tok, part)], axis=1)

    w_grad = lax.dot_general(
        rows, dcache, (((0,), (0,)), ((), ())), preferred_element_type=jnp.float32
    ).astype(jnp.bfloat16)
    w_grad = jnp.transpose(
        w_grad.reshape(sections, shards, blk, auxes, part), (1, 0, 3, 2, 4)
    ).reshape(shards, peers, blk, part)
    w_sum = lax.psum_scatter(w_grad, "dp", scatter_dimension=0, tiled=True)
    w_back = lax.all_to_all(w_sum.reshape(peers, blk, part), both, split_axis=0, concat_axis=0, tiled=True)
    grad_predictors = (
        w_back.reshape(sections, auxes, blk, part).swapaxes(1, 2).reshape(predictors.shape)
    ).astype(jnp.float32)

    r_term = lax.dot_general(
        dcache, weight, (((1,), (1,)), ((), ())), preferred_element_type=jnp.float32
    ).astype(jnp.bfloat16)
    r_send = jnp.swapaxes(
        r_term.reshape(sections, rows_each, auxes, feats), 1, 2
    ).reshape(peers, rows_each, feats)
    r_back = lax.all_to_all(r_send, both, split_axis=0, concat_axis=0, tiled=True)
    r_sum = jnp.sum(r_back.reshape(sections, auxes, rows_each, feats).astype(jnp.float32), axis=1)
    grad_rows = r_sum.astype(jnp.bfloat16).reshape(aux_rows.shape)
    return (grad_rows, grad_predictors)


def solution(mesh):
    return jax.shard_map(
        per_device,
        mesh=mesh,
        in_specs=(
            P(None, "dp", "section", "aux"),
            P("aux", None, "section", "dp", None, None),
            P("section", "dp", "aux"),
            P("section", "dp", "aux"),
            P("dp", None),
        ),
        out_specs=(P(None, "dp", "section", "aux"), P("aux", None, "section", "dp", None, None)),
        check_vma=False,
    )
```

```python
import math

import jax
import jax.numpy as jnp
from jax import lax
from jax.experimental import pallas as pl
from jax.experimental.pallas import tpu as pltpu
from jax.sharding import PartitionSpec as P

HEAD_DIM = 128
F32 = jnp.float32
BF16 = jnp.bfloat16
W_SCALE = 2.0**18


def dot(a, b, dims):
    return lax.dot_general(a, b, (dims, ((), ())), preferred_element_type=F32)


NN = ((1,), (0,))
NT = ((1,), (1,))
TN = ((0,), (0,))


def order_weights(w_ref, wk_ref, wv_ref):
    shards, sections, two_blk, part = w_ref.shape
    blk = two_blk // 2
    for pair in range(shards // 2):
        one = w_ref[2 * pair].astype(F32)
        two = w_ref[2 * pair + 1].astype(F32)
        keys = jnp.concatenate([one[:, :blk], two[:, :blk]], axis=1)
        values = jnp.concatenate([one[:, blk:], two[:, blk:]], axis=1)
        wk_ref[:, pair] = keys.astype(BF16)
        wv_ref[:, pair] = values.astype(BF16)


def attend_kernel(me_ref, w_ref, r_ref, docr_ref, docc_ref, q_any, g_any,
                  dw_ref, dc_ref, wk_ref, wv_ref,
                  q_ref, g_ref, rows_ref, bias_ref, dk_ref, dv_ref, sems):
    shards, sections, two_blk, part = w_ref.shape
    blk = two_blk // 2
    tok = q_ref.shape[0]
    half = tok // 2
    feats = r_ref.shape[2]
    each = tok // sections
    auxes = r_ref.shape[1] // each
    width = sections * shards * blk

    q_copy = pltpu.make_async_copy(q_any, q_ref, sems.at[0])
    g_copy = pltpu.make_async_copy(g_any, g_ref, sems.at[1])
    q_copy.start()
    g_copy.start()
    order_weights(w_ref, wk_ref, wv_ref)
    for a in range(auxes):
        piece = r_ref[:, a * each:(a + 1) * each, :].astype(F32)
        rows_ref[:, a * feats:(a + 1) * feats] = piece.reshape(tok, feats).astype(BF16)

    rows = rows_ref[...]
    keys = dot(rows, wk_ref[...].reshape(width, part), NN).astype(BF16)
    values = dot(rows, wv_ref[...].reshape(width, part), NN).astype(BF16)

    j_at = lax.broadcasted_iota(jnp.int32, (tok, tok), 0)
    i_at = lax.broadcasted_iota(jnp.int32, (tok, tok), 1)
    seen = (docc_ref[...] == docr_ref[...]) & (j_at <= i_at)
    bias_ref[...] = jnp.where(seen, 0.0, -1e30).astype(F32)

    scale = 1.0 / math.sqrt(HEAD_DIM)
    to_two = scale * math.log2(math.e)
    kv_heads = part // HEAD_DIM
    group = q_ref.shape[1] // part

    def softmax(s, bias):
        t = s * to_two + bias
        e = jnp.exp2(t - jnp.max(t, axis=0, keepdims=True))
        return e * (1.0 / jnp.sum(e, axis=0, keepdims=True))

    q_copy.wait()
    g_copy.wait()
    for h in range(kv_heads):
        k_h = keys[:, h * HEAD_DIM:(h + 1) * HEAD_DIM]
        v_h = values[:, h * HEAD_DIM:(h + 1) * HEAD_DIM]
        v_t = v_h.astype(F32).T.astype(BF16)
        dk_ref[...] = jnp.zeros_like(dk_ref)
        dv_ref[...] = jnp.zeros_like(dv_ref)

        def one_head(at):
            cols = pl.ds(pl.multiple_of(at * HEAD_DIM, HEAD_DIM), HEAD_DIM)
            q = q_ref[:, cols]
            goal_t = g_ref[:, cols].astype(F32).T
            s = dot(k_h, q, NT)
            p_a = softmax(s[:half, :half], bias_ref[:half, :half])
            p_b = softmax(s[:, half:], bias_ref[:, half:])
            low = jnp.concatenate([p_a.astype(BF16), jnp.zeros((half, half), BF16)], axis=0)
            p = jnp.concatenate([low, p_b.astype(BF16)], axis=1)
            out_t = dot(v_t, p, NN)
            dout = out_t - goal_t
            dout_b = dout.astype(BF16)
            delta = jnp.sum(dout * out_t, axis=0, keepdims=True)
            dp = dot(v_h, dout_b, NN)
            ds_a = (p_a * (dp[:half, :half] - delta[:, :half]) * scale).astype(BF16)
            ds_b = (p_b * (dp[:, half:] - delta[:, half:]) * scale).astype(BF16)
            ds_low = jnp.concatenate([ds_a, jnp.zeros((half, half), BF16)], axis=0)
            ds = jnp.concatenate([ds_low, ds_b], axis=1)
            return dot(ds, q, NN), dot(p, dout_b, NT)

        def two_heads(step, _):
            dk0, dv0 = one_head(h * group + 2 * step)
            dk1, dv1 = one_head(h * group + 2 * step + 1)
            dk_ref[...] += dk0 + dk1
            dv_ref[...] += dv0 + dv1
            return 0

        lax.fori_loop(0, group // 2, two_heads, 0)
        dc_ref[:, h * HEAD_DIM:(h + 1) * HEAD_DIM] = dk_ref[...].astype(BF16)
        dc_ref[:, part + h * HEAD_DIM:part + (h + 1) * HEAD_DIM] = dv_ref[...].astype(BF16)

    me = me_ref[0]
    dcache = dc_ref[...]
    step_rows = 4 * shards * blk
    for at in range(sections // 4):
        x = rows_ref[:, at * step_rows:(at + 1) * step_rows]
        full = dot(x, dcache, TN).reshape(4, shards, blk, 2 * part)
        for d in range(shards):
            both = jnp.concatenate([full[:, d, :, :part], full[:, d, :, part:]], axis=1)
            dw_ref[lax.rem(d + shards - me, shards), at * 4:(at + 1) * 4] = both.astype(BF16)


def rows_kernel(w_ref, dc_ref, out_ref, wk_ref, wv_ref):
    shards, sections, two_blk, part = w_ref.shape
    width = sections * shards * two_blk // 2
    feats = out_ref.shape[2]
    auxes = width // feats
    each = dc_ref.shape[0] // sections
    order_weights(w_ref, wk_ref, wv_ref)
    w_k = wk_ref[...].reshape(width, part)
    w_v = wv_ref[...].reshape(width, part)
    for a in range(auxes):
        span = slice(a * feats, (a + 1) * feats)
        term = dot(dc_ref[:, :part], w_k[span], NT) + dot(dc_ref[:, part:], w_v[span], NT)
        out_ref[:, a * each:(a + 1) * each, :] = term.reshape(sections, each, feats).astype(BF16)


def double_kernel(x_ref, out_ref):
    for a in range(out_ref.shape[1]):
        out_ref[:, a] = x_ref[...]


def double(x, auxes):
    return pl.pallas_call(
        double_kernel,
        out_shape=jax.ShapeDtypeStruct((x.shape[0], auxes) + x.shape[1:], x.dtype),
        in_specs=[whole()],
        out_specs=whole(),
        compiler_params=pltpu.CompilerParams(vmem_limit_bytes=8 * 2**20),
        cost_estimate=pl.CostEstimate(flops=0, bytes_accessed=2 * (1 + auxes) * x.size, transcendentals=0),
        name="double",
    )(x)


def whole(space=pltpu.VMEM):
    return pl.BlockSpec(memory_space=space)


def attend(me, w_all, r_in, queries, goal, docs):
    shards, sections, two_blk, part = w_all.shape
    tok = queries.shape[0]
    width = sections * shards * two_blk // 2
    ordered = (sections, shards // 2, two_blk, part)
    return pl.pallas_call(
        attend_kernel,
        out_shape=(
            jax.ShapeDtypeStruct(w_all.shape, BF16),
            jax.ShapeDtypeStruct((tok, 2 * part), BF16),
        ),
        in_specs=[whole(pltpu.SMEM)] + [whole()] * 4 + [whole(pl.ANY)] * 2,
        out_specs=(whole(),) * 2,
        scratch_shapes=[
            pltpu.VMEM(ordered, BF16),
            pltpu.VMEM(ordered, BF16),
            pltpu.VMEM(queries.shape, BF16),
            pltpu.VMEM(queries.shape, BF16),
            pltpu.VMEM((tok, width), BF16),
            pltpu.VMEM((tok, tok), F32),
            pltpu.VMEM((tok, HEAD_DIM), F32),
            pltpu.VMEM((tok, HEAD_DIM), F32),
            pltpu.SemaphoreType.DMA((2,)),
        ],
        compiler_params=pltpu.CompilerParams(vmem_limit_bytes=16 * 2**20),
        cost_estimate=pl.CostEstimate(
            flops=2 * (2 * tok * width * 2 * part + 5 * tok * tok * queries.shape[1]),
            bytes_accessed=9 * 2**20,
            transcendentals=tok * tok * queries.shape[1] // HEAD_DIM,
        ),
        name="attend",
    )(me, w_all, r_in, docs.reshape(1, tok), docs.reshape(tok, 1), queries, goal)


def row_terms(w_all, dcache, feats):
    shards, sections, two_blk, part = w_all.shape
    tok = dcache.shape[0]
    width = sections * shards * two_blk // 2
    ordered = (sections, shards // 2, two_blk, part)
    return pl.pallas_call(
        rows_kernel,
        out_shape=jax.ShapeDtypeStruct((sections, tok // sections * (width // feats), feats), BF16),
        in_specs=[whole()] * 2,
        out_specs=whole(),
        scratch_shapes=[pltpu.VMEM(ordered, BF16), pltpu.VMEM(ordered, BF16)],
        compiler_params=pltpu.CompilerParams(vmem_limit_bytes=10 * 2**20),
        cost_estimate=pl.CostEstimate(
            flops=4 * tok * width * part, bytes_accessed=4 * 2**20, transcendentals=0
        ),
        name="row_terms",
    )(w_all, dcache)


def reduce_ring(terms, axis):
    n = lax.axis_size(axis)
    ahead = [(i, (i + 1) % n) for i in range(n)]
    back = [(i, (i - 1) % n) for i in range(n)]
    far = n // 2
    up = terms[far]
    for k in range(far - 1, -1, -1):
        up = lax.ppermute(up, axis, ahead)
        if k:
            up = (up.astype(F32) + terms[k].astype(F32)).astype(BF16)
    total = terms[0].astype(F32) + up.astype(F32)
    if n - far > 1:
        down = terms[far + 1]
        for k in range(far + 2, n):
            down = lax.ppermute(down, axis, back)
            down = (down.astype(F32) + terms[k].astype(F32)).astype(BF16)
        down = lax.ppermute(down, axis, back)
        total = total + down.astype(F32)
    return total.astype(BF16)


def per_device(aux_rows, predictors, queries, target, lengths):
    sections = lax.axis_size("section")
    auxes = lax.axis_size("aux")
    shards = lax.axis_size("dp")
    both = ("section", "aux")
    peers = sections * auxes
    blk, width = predictors.shape[4:]
    part = width // auxes
    rows_each, feats = aux_rows.shape[2:]
    tok = sections * rows_each

    w_out = predictors.reshape(sections, blk, auxes, part).swapaxes(1, 2).reshape(peers, blk, part)
    w_out = (w_out * W_SCALE).astype(jnp.float16)
    w_in = lax.all_to_all(w_out, both, split_axis=0, concat_axis=0, tiled=True)

    r_out = double(aux_rows.reshape(sections, rows_each, feats), auxes).reshape(
        peers, rows_each, feats
    )
    w_in, r_out = lax.optimization_barrier((w_in, r_out))
    r_in = lax.all_to_all(r_out, both, split_axis=0, concat_axis=0, tiled=True)
    r_in = r_in.reshape(sections, auxes * rows_each, feats)

    w_all = lax.all_gather(w_in, "dp", axis=0)
    w_all = (w_all.astype(F32) * (1.0 / W_SCALE)).astype(BF16)
    w_all = w_all.reshape(shards, sections, auxes * blk, part)

    ends = jnp.cumsum(lengths[0])
    pos = jnp.arange(tok, dtype=jnp.int32)
    docs = jnp.sum((pos[:, None] >= ends[None, :]).astype(jnp.int32), axis=1)
    me = lax.axis_index("dp").astype(jnp.int32).reshape(1)
    dw, dcache = attend(me, w_all, r_in, queries[0], target[0], docs)

    r_send = row_terms(w_all, dcache, feats).reshape(peers, rows_each, feats)
    r_back = lax.all_to_all(r_send, both, split_axis=0, concat_axis=0, tiled=True)
    w_sum = reduce_ring([dw[k] for k in range(shards)], "dp")
    w_sum, r_back = lax.optimization_barrier((w_sum, r_back))
    w_back = lax.all_to_all(w_sum.reshape(peers, blk, part), both, split_axis=0, concat_axis=0, tiled=True)
    grad_predictors = (
        w_back.reshape(sections, auxes, blk, part).swapaxes(1, 2).reshape(predictors.shape)
    ).astype(F32)
    r_sum = jnp.sum(r_back.reshape(sections, auxes, rows_each, feats).astype(F32), axis=1)
    grad_rows = r_sum.astype(BF16).reshape(aux_rows.shape)
    return (grad_rows, grad_predictors)


def solution(mesh):
    return jax.shard_map(
        per_device,
        mesh=mesh,
        in_specs=(
            P(None, "dp", "section", "aux"),
            P("aux", None, "section", "dp", None, None),
            P("section", "dp", "aux"),
            P("section", "dp", "aux"),
            P("dp", None),
        ),
        out_specs=(P(None, "dp", "section", "aux"), P("aux", None, "section", "dp", None, None)),
        check_vma=False,
    )
```

```python
import functools
import math

import jax
import jax.numpy as jnp
from jax import lax
from jax.experimental import pallas as pl
from jax.experimental.pallas import tpu as pltpu
from jax.sharding import PartitionSpec as P

HEAD_DIM = 128
F32 = jnp.float32
BF16 = jnp.bfloat16
W_SCALE = 2.0**18
HOP_FLOPS = 16 * 10**9


def dot(a, b, dims):
    return lax.dot_general(a, b, (dims, ((), ())), preferred_element_type=F32)


NN = ((1,), (0,))
NT = ((1,), (1,))
TN = ((0,), (0,))


def order_weights(w_ref, wk_ref, wv_ref):
    shards, sections, two_blk, part = w_ref.shape
    blk = two_blk // 2
    for pair in range(shards // 2):
        one = w_ref[2 * pair].astype(F32)
        two = w_ref[2 * pair + 1].astype(F32)
        keys = jnp.concatenate([one[:, :blk], two[:, :blk]], axis=1)
        values = jnp.concatenate([one[:, blk:], two[:, blk:]], axis=1)
        wk_ref[:, pair] = keys.astype(BF16)
        wv_ref[:, pair] = values.astype(BF16)


def attend_kernel(groups, me_ref, w_ref, r_ref, q_ref, g_ref, docr_ref, docc_ref, *refs):
    part_refs, (dc_ref, wk_ref, wv_ref, rows_ref, bias_ref, dw_ref) = refs[:-6], refs[-6:]
    shards, sections, two_blk, part = w_ref.shape
    blk = two_blk // 2
    tok = q_ref.shape[0]
    half = tok // 2
    feats = r_ref.shape[2]
    each = tok // sections
    auxes = r_ref.shape[1] // each
    width = sections * shards * blk

    order_weights(w_ref, wk_ref, wv_ref)
    for a in range(auxes):
        piece = r_ref[:, a * each:(a + 1) * each, :].astype(F32)
        rows_ref[:, a * feats:(a + 1) * feats] = piece.reshape(tok, feats).astype(BF16)

    rows = rows_ref[...]
    keys = dot(rows, wk_ref[...].reshape(width, part), NN).astype(BF16)
    values = dot(rows, wv_ref[...].reshape(width, part), NN).astype(BF16)

    j_at = lax.broadcasted_iota(jnp.int32, (tok, tok), 0)
    i_at = lax.broadcasted_iota(jnp.int32, (tok, tok), 1)
    seen = (docc_ref[...] == docr_ref[...]) & (j_at <= i_at)
    bias_ref[...] = jnp.where(seen, 0.0, -1e30).astype(F32)

    scale = 1.0 / math.sqrt(HEAD_DIM)
    to_two = scale * math.log2(math.e)
    kv_heads = part // HEAD_DIM
    group = q_ref.shape[1] // part

    def softmax(s, bias):
        t = s * to_two + bias
        e = jnp.exp2(t - jnp.max(t, axis=0, keepdims=True))
        return e * (1.0 / jnp.sum(e, axis=0, keepdims=True))

    def whole_square(x_a, x_b):
        low = jnp.concatenate([x_a, jnp.zeros((half, half), BF16)], axis=0)
        return jnp.concatenate([low, x_b], axis=1)

    for h in range(kv_heads):
        k_h = keys[:, h * HEAD_DIM:(h + 1) * HEAD_DIM]
        v_h = values[:, h * HEAD_DIM:(h + 1) * HEAD_DIM]
        v_t = v_h.astype(F32).T.astype(BF16)

        def heads_of(h, k_h, v_h, v_t):
            at = [h * group + n for n in range(group)]
            cols = [pl.ds(pl.multiple_of(n * HEAD_DIM, HEAD_DIM), HEAD_DIM) for n in at]
            q = [q_ref[:, c] for c in cols]
            s = [dot(k_h, x, NT) for x in q]
            goal = [g_ref[:, c].T.astype(F32) for c in cols]
            p_a = [softmax(x[:half, :half], bias_ref[:half, :half]) for x in s]
            p_b = [softmax(x[:, half:], bias_ref[:, half:]) for x in s]
            p = [whole_square(x.astype(BF16), y.astype(BF16)) for x, y in zip(p_a, p_b)]
            out = [dot(v_t, x, NN) for x in p]
            dout = [x - y for x, y in zip(out, goal)]
            dout_b = [x.astype(BF16) for x in dout]
            dp = [dot(v_h, x, NN) for x in dout_b]
            delta = [jnp.sum(x * y, axis=0, keepdims=True) for x, y in zip(dout, out)]
            ds_a = [
                (x * (y[:half, :half] - z[:, :half]) * scale).astype(BF16)
                for x, y, z in zip(p_a, dp, delta)
            ]
            ds_b = [
                (x * (y[:, half:] - z[:, half:]) * scale).astype(BF16)
                for x, y, z in zip(p_b, dp, delta)
            ]
            ds = [whole_square(x, y) for x, y in zip(ds_a, ds_b)]
            dv = sum(dot(x, y, NT) for x, y in zip(p, dout_b))
            dk = sum(dot(x, y, NN) for x, y in zip(ds, q))
            return dk, dv

        dk, dv = heads_of(h, k_h, v_h, v_t)
        dc_ref[:, h * HEAD_DIM:(h + 1) * HEAD_DIM] = dk.astype(BF16)
        dc_ref[:, part + h * HEAD_DIM:part + (h + 1) * HEAD_DIM] = dv.astype(BF16)

    me = me_ref[0]
    dcache = dc_ref[...]
    step_rows = 4 * shards * blk
    for at in range(sections // 4):
        x = rows_ref[:, at * step_rows:(at + 1) * step_rows]
        full = dot(x, dcache, TN).reshape(4, shards, blk, 2 * part)
        for d in range(shards):
            both = jnp.concatenate([full[:, d, :, :part], full[:, d, :, part:]], axis=1)
            dw_ref[lax.rem(d + shards - me, shards), at * 4:(at + 1) * 4] = both.astype(BF16)
    for group_at, ref in zip(groups, part_refs):
        for slot, k in enumerate(group_at):
            ref[slot] = dw_ref[k]


def rows_kernel(w_ref, dc_ref, out_ref, wk_ref, wv_ref):
    shards, sections, two_blk, part = w_ref.shape
    width = sections * shards * two_blk // 2
    feats = out_ref.shape[2]
    auxes = width // feats
    each = dc_ref.shape[0] // sections
    order_weights(w_ref, wk_ref, wv_ref)
    w_k = wk_ref[...].reshape(width, part)
    w_v = wv_ref[...].reshape(width, part)
    for a in range(auxes):
        span = slice(a * feats, (a + 1) * feats)
        term = dot(dc_ref[:, :part], w_k[span], NT) + dot(dc_ref[:, part:], w_v[span], NT)
        out_ref[:, a * each:(a + 1) * each, :] = term.reshape(sections, each, feats).astype(BF16)


def double_kernel(x_ref, out_ref):
    for a in range(out_ref.shape[1]):
        out_ref[:, a] = x_ref[...]


def double(x, auxes):
    return pl.pallas_call(
        double_kernel,
        out_shape=jax.ShapeDtypeStruct((x.shape[0], auxes) + x.shape[1:], x.dtype),
        in_specs=[whole()],
        out_specs=whole(),
        compiler_params=pltpu.CompilerParams(vmem_limit_bytes=8 * 2**20),
        cost_estimate=pl.CostEstimate(flops=0, bytes_accessed=2 * (1 + auxes) * x.size, transcendentals=0),
        name="double",
    )(x)


def whole(space=pltpu.VMEM):
    return pl.BlockSpec(memory_space=space)


def attend(me, w_all, r_in, queries, goal, docs, groups):
    shards, sections, two_blk, part = w_all.shape
    tok = queries.shape[0]
    width = sections * shards * two_blk // 2
    ordered = (sections, shards // 2, two_blk, part)
    return pl.pallas_call(
        functools.partial(attend_kernel, groups),
        out_shape=tuple(
            jax.ShapeDtypeStruct((len(group),) + w_all.shape[1:], BF16) for group in groups
        )
        + (jax.ShapeDtypeStruct((tok, 2 * part), BF16),),
        in_specs=[whole(pltpu.SMEM)] + [whole()] * 6,
        out_specs=(whole(),) * (len(groups) + 1),
        scratch_shapes=[
            pltpu.VMEM(ordered, BF16),
            pltpu.VMEM(ordered, BF16),
            pltpu.VMEM((tok, width), BF16),
            pltpu.VMEM((tok, tok), F32),
            pltpu.VMEM(w_all.shape, BF16),
        ],
        compiler_params=pltpu.CompilerParams(vmem_limit_bytes=16 * 2**20),
        cost_estimate=pl.CostEstimate(
            flops=2 * (2 * tok * width * 2 * part + 5 * tok * tok * queries.shape[1]),
            bytes_accessed=9 * 2**20,
            transcendentals=tok * tok * queries.shape[1] // HEAD_DIM,
        ),
        name="attend",
    )(me, w_all, r_in, queries, goal, docs.reshape(1, tok), docs.reshape(tok, 1))


def row_terms(w_all, dcache, feats):
    shards, sections, two_blk, part = w_all.shape
    tok = dcache.shape[0]
    width = sections * shards * two_blk // 2
    ordered = (sections, shards // 2, two_blk, part)
    return pl.pallas_call(
        rows_kernel,
        out_shape=jax.ShapeDtypeStruct((sections, tok // sections * (width // feats), feats), BF16),
        in_specs=[whole()] * 2,
        out_specs=whole(),
        scratch_shapes=[pltpu.VMEM(ordered, BF16), pltpu.VMEM(ordered, BF16)],
        compiler_params=pltpu.CompilerParams(vmem_limit_bytes=7 * 2**20),
        cost_estimate=pl.CostEstimate(
            flops=4 * tok * width * part, bytes_accessed=4 * 2**20, transcendentals=0
        ),
        name="row_terms",
    )(w_all, dcache)


def add_kernel(*refs):
    total = refs[0][0].astype(F32)
    for ref in refs[1:-1]:
        total = total + ref[0].astype(F32)
    refs[-1][...] = total.astype(refs[-1].dtype).reshape(refs[-1].shape)


def add_term(*parts, flops=0, dtype=BF16):
    shape = parts[0][0].shape[1:]

    def spec(at):
        return pl.BlockSpec((1,) + shape, lambda i: (at,) + (0,) * len(shape))

    return pl.pallas_call(
        add_kernel,
        grid=(1,),
        out_shape=jax.ShapeDtypeStruct((1,) + shape, dtype),
        in_specs=[spec(at) for _, at in parts],
        out_specs=spec(0),
        compiler_params=pltpu.CompilerParams(vmem_limit_bytes=8 * 2**20),
        cost_estimate=pl.CostEstimate(flops=flops, bytes_accessed=2**20, transcendentals=0),
        name="add_term",
    )(*[array for array, _ in parts])


def reduce_groups(n):
    return [(0, 2, 6), (1, 3), (7, 5), (4,)] if n == 8 else [(0,), (1,)]


def reduce_scatter(parts, axis):
    n = lax.axis_size(axis)

    def send(x, places):
        return lax.ppermute(x, axis, [(i, (i + places) % n) for i in range(n)])

    if n == 2:
        return add_term((parts[0], 0), (send(parts[1], 1), 0))
    kept, up, down, far = parts
    up, down, far = lax.optimization_barrier((send(up, 1), send(down, -1), far))
    far = send(far, 4)
    up_two = send(add_term((kept, 1), (up, 1)), 2)
    down_two = send(add_term((kept, 2), (down, 1)), -2)
    base = add_term((kept, 0), (up, 0), (down, 0), (far, 0), dtype=F32)
    return add_term((base, 0), (up_two, 0), (down_two, 0), flops=HOP_FLOPS)


def per_device(aux_rows, predictors, queries, target, lengths):
    sections = lax.axis_size("section")
    auxes = lax.axis_size("aux")
    shards = lax.axis_size("dp")
    both = ("section", "aux")
    peers = sections * auxes
    blk, width = predictors.shape[4:]
    part = width // auxes
    rows_each, feats = aux_rows.shape[2:]
    tok = sections * rows_each

    w_out = predictors.reshape(sections, blk, auxes, part).swapaxes(1, 2).reshape(peers, blk, part)
    w_out = (w_out * W_SCALE).astype(jnp.float16)
    w_in = lax.all_to_all(w_out, both, split_axis=0, concat_axis=0, tiled=True)

    r_out = double(aux_rows.reshape(sections, rows_each, feats), auxes).reshape(
        peers, rows_each, feats
    )
    w_in, r_out = lax.optimization_barrier((w_in, r_out))
    r_in = lax.all_to_all(r_out, both, split_axis=0, concat_axis=0, tiled=True)
    r_in = r_in.reshape(sections, auxes * rows_each, feats)

    w_all = lax.all_gather(w_in, "dp", axis=0)
    w_all = (w_all.astype(F32) * (1.0 / W_SCALE)).astype(BF16)
    w_all = w_all.reshape(shards, sections, auxes * blk, part)

    ends = jnp.cumsum(lengths[0])
    pos = jnp.arange(tok, dtype=jnp.int32)
    docs = jnp.sum((pos[:, None] >= ends[None, :]).astype(jnp.int32), axis=1)
    me = lax.axis_index("dp").astype(jnp.int32).reshape(1)
    *dw, dcache = attend(me, w_all, r_in, queries[0], target[0], docs, reduce_groups(shards))

    r_send = row_terms(w_all, dcache, feats).reshape(peers, rows_each, feats)
    r_back = lax.all_to_all(r_send, both, split_axis=0, concat_axis=0, tiled=True)
    w_sum = reduce_scatter(dw, "dp")
    w_sum, r_back = lax.optimization_barrier((w_sum, r_back))
    w_back = lax.all_to_all(w_sum.reshape(peers, blk, part), both, split_axis=0, concat_axis=0, tiled=True)
    grad_predictors = (
        w_back.reshape(sections, auxes, blk, part).swapaxes(1, 2).reshape(predictors.shape)
    ).astype(F32)
    r_sum = jnp.sum(r_back.reshape(sections, auxes, rows_each, feats).astype(F32), axis=1)
    grad_rows = r_sum.astype(BF16).reshape(aux_rows.shape)
    return (grad_rows, grad_predictors)


def solution(mesh):
    return jax.shard_map(
        per_device,
        mesh=mesh,
        in_specs=(
            P(None, "dp", "section", "aux"),
            P("aux", None, "section", "dp", None, None),
            P("section", "dp", "aux"),
            P("section", "dp", "aux"),
            P("dp", None),
        ),
        out_specs=(P(None, "dp", "section", "aux"), P("aux", None, "section", "dp", None, None)),
        check_vma=False,
    )
```

```python
import functools
import math

import jax
import jax.numpy as jnp
from jax import lax
from jax.experimental import pallas as pl
from jax.experimental.pallas import tpu as pltpu
from jax.sharding import PartitionSpec as P

HEAD_DIM = 128
F32 = jnp.float32
BF16 = jnp.bfloat16
W_SCALE = 2.0**18
HOP_FLOPS = 16 * 10**9


def dot(a, b, dims):
    return lax.dot_general(a, b, (dims, ((), ())), preferred_element_type=F32)


NN = ((1,), (0,))
NT = ((1,), (1,))
TN = ((0,), (0,))


def order_weights(w_ref, wk_ref, wv_ref):
    shards, sections, two_blk, part = w_ref.shape
    blk = two_blk // 2
    for pair in range(shards // 2):
        one = w_ref[2 * pair].astype(F32)
        two = w_ref[2 * pair + 1].astype(F32)
        keys = jnp.concatenate([one[:, :blk], two[:, :blk]], axis=1)
        values = jnp.concatenate([one[:, blk:], two[:, blk:]], axis=1)
        wk_ref[:, pair] = keys.astype(BF16)
        wv_ref[:, pair] = values.astype(BF16)


def project_kernel(w_ref, r_ref, cache_ref, rows_ref, wk_ref, wv_ref):
    shards, sections, two_blk, part = w_ref.shape
    width = sections * shards * two_blk // 2
    tok = rows_ref.shape[0]
    feats = r_ref.shape[2]
    each = tok // sections

    order_weights(w_ref, wk_ref, wv_ref)
    for a in range(width // feats):
        piece = r_ref[:, a * each:(a + 1) * each, :].astype(F32)
        rows_ref[:, a * feats:(a + 1) * feats] = piece.reshape(tok, feats).astype(BF16)
    rows = rows_ref[...]
    cache_ref[:, :part] = dot(rows, wk_ref[...].reshape(width, part), NN).astype(BF16)
    cache_ref[:, part:] = dot(rows, wv_ref[...].reshape(width, part), NN).astype(BF16)


def attend_kernel(groups, me_ref, cache_ref, rows_ref, q_ref, g_ref, docr_ref, docc_ref, *refs):
    part_refs, (dc_ref, bias_ref, dw_ref) = refs[:-3], refs[-3:]
    shards, sections, two_blk, part = dw_ref.shape
    blk = two_blk // 2
    tok = q_ref.shape[0]
    half = tok // 2
    keys = cache_ref[:, :part]
    values = cache_ref[:, part:]

    j_at = lax.broadcasted_iota(jnp.int32, (tok, tok), 0)
    i_at = lax.broadcasted_iota(jnp.int32, (tok, tok), 1)
    seen = (docc_ref[...] == docr_ref[...]) & (j_at <= i_at)
    bias_ref[...] = jnp.where(seen, 0.0, -1e30).astype(F32)

    scale = 1.0 / math.sqrt(HEAD_DIM)
    to_two = scale * math.log2(math.e)
    kv_heads = part // HEAD_DIM
    group = q_ref.shape[1] // part

    def softmax(s, bias):
        t = s * to_two + bias
        e = jnp.exp2(t - jnp.max(t, axis=0, keepdims=True))
        return e * (1.0 / jnp.sum(e, axis=0, keepdims=True))

    def whole_square(x_a, x_b):
        low = jnp.concatenate([x_a, jnp.zeros((half, half), BF16)], axis=0)
        return jnp.concatenate([low, x_b], axis=1)

    for h in range(kv_heads):
        k_h = keys[:, h * HEAD_DIM:(h + 1) * HEAD_DIM]
        v_h = values[:, h * HEAD_DIM:(h + 1) * HEAD_DIM]
        v_t = v_h.astype(F32).T.astype(BF16)

        def heads_of(h, k_h, v_h, v_t):
            at = [h * group + n for n in range(group)]
            cols = [pl.ds(pl.multiple_of(n * HEAD_DIM, HEAD_DIM), HEAD_DIM) for n in at]
            q = [q_ref[:, c] for c in cols]
            s = [dot(k_h, x, NT) for x in q]
            goal = [g_ref[:, c].T.astype(F32) for c in cols]
            p_a = [softmax(x[:half, :half], bias_ref[:half, :half]) for x in s]
            p_b = [softmax(x[:, half:], bias_ref[:, half:]) for x in s]
            p = [whole_square(x.astype(BF16), y.astype(BF16)) for x, y in zip(p_a, p_b)]
            out = [dot(v_t, x, NN) for x in p]
            dout = [x - y for x, y in zip(out, goal)]
            dout_b = [x.astype(BF16) for x in dout]
            dp = [dot(v_h, x, NN) for x in dout_b]
            delta = [jnp.sum(x * y, axis=0, keepdims=True) for x, y in zip(dout, out)]
            ds_a = [
                (x * (y[:half, :half] - z[:, :half]) * scale).astype(BF16)
                for x, y, z in zip(p_a, dp, delta)
            ]
            ds_b = [
                (x * (y[:, half:] - z[:, half:]) * scale).astype(BF16)
                for x, y, z in zip(p_b, dp, delta)
            ]
            ds = [whole_square(x, y) for x, y in zip(ds_a, ds_b)]
            dv = sum(dot(x, y, NT) for x, y in zip(p, dout_b))
            dk = sum(dot(x, y, NN) for x, y in zip(ds, q))
            return dk, dv

        dk, dv = heads_of(h, k_h, v_h, v_t)
        dc_ref[:, h * HEAD_DIM:(h + 1) * HEAD_DIM] = dk.astype(BF16)
        dc_ref[:, part + h * HEAD_DIM:part + (h + 1) * HEAD_DIM] = dv.astype(BF16)

    me = me_ref[0]
    dcache = dc_ref[...]
    step_rows = 4 * shards * blk
    for at in range(sections // 4):
        x = rows_ref[:, at * step_rows:(at + 1) * step_rows]
        full = dot(x, dcache, TN).reshape(4, shards, blk, 2 * part)
        for d in range(shards):
            both = jnp.concatenate([full[:, d, :, :part], full[:, d, :, part:]], axis=1)
            dw_ref[lax.rem(d + shards - me, shards), at * 4:(at + 1) * 4] = both.astype(BF16)
    for group_at, ref in zip(groups, part_refs):
        for slot, k in enumerate(group_at):
            ref[slot] = dw_ref[k]


def rows_kernel(wk_ref, wv_ref, dc_ref, out_ref):
    sections, _, _, part = wk_ref.shape
    width = wk_ref.size // part
    feats = out_ref.shape[2]
    each = dc_ref.shape[0] // sections
    w_k = wk_ref[...].reshape(width, part)
    w_v = wv_ref[...].reshape(width, part)
    for a in range(width // feats):
        span = slice(a * feats, (a + 1) * feats)
        term = dot(dc_ref[:, :part], w_k[span], NT) + dot(dc_ref[:, part:], w_v[span], NT)
        out_ref[:, a * each:(a + 1) * each, :] = term.reshape(sections, each, feats).astype(BF16)


def double_kernel(x_ref, out_ref):
    for a in range(out_ref.shape[1]):
        out_ref[:, a] = x_ref[...]


def double(x, auxes):
    return pl.pallas_call(
        double_kernel,
        out_shape=jax.ShapeDtypeStruct((x.shape[0], auxes) + x.shape[1:], x.dtype),
        in_specs=[whole()],
        out_specs=whole(),
        compiler_params=pltpu.CompilerParams(vmem_limit_bytes=8 * 2**20),
        cost_estimate=pl.CostEstimate(flops=0, bytes_accessed=2 * (1 + auxes) * x.size, transcendentals=0),
        name="double",
    )(x)


def whole(space=pltpu.VMEM):
    return pl.BlockSpec(memory_space=space)


def project(w_all, r_in):
    shards, sections, two_blk, part = w_all.shape
    width = sections * shards * two_blk // 2
    tok = r_in.size // width
    ordered = jax.ShapeDtypeStruct((sections, shards // 2, two_blk, part), BF16)
    return pl.pallas_call(
        project_kernel,
        out_shape=(
            jax.ShapeDtypeStruct((tok, 2 * part), BF16),
            jax.ShapeDtypeStruct((tok, width), BF16),
            ordered,
            ordered,
        ),
        in_specs=[whole()] * 2,
        out_specs=(whole(),) * 4,
        compiler_params=pltpu.CompilerParams(vmem_limit_bytes=12 * 2**20),
        cost_estimate=pl.CostEstimate(
            flops=4 * tok * width * part, bytes_accessed=6 * 2**20, transcendentals=0
        ),
        name="project",
    )(w_all, r_in)


def attend(me, cache, rows, queries, goal, docs, groups, term):
    tok = queries.shape[0]
    return pl.pallas_call(
        functools.partial(attend_kernel, groups),
        out_shape=tuple(jax.ShapeDtypeStruct((len(group),) + term, BF16) for group in groups)
        + (jax.ShapeDtypeStruct(cache.shape, BF16),),
        in_specs=[whole(pltpu.SMEM)] + [whole()] * 6,
        out_specs=(whole(),) * (len(groups) + 1),
        scratch_shapes=[
            pltpu.VMEM((tok, tok), F32),
            pltpu.VMEM((sum(len(group) for group in groups),) + term, BF16),
        ],
        compiler_params=pltpu.CompilerParams(vmem_limit_bytes=16 * 2**20),
        cost_estimate=pl.CostEstimate(
            flops=2 * (rows.size * cache.shape[1] + 5 * tok * queries.size),
            bytes_accessed=6 * 2**20,
            transcendentals=tok * queries.size // HEAD_DIM,
        ),
        name="attend",
    )(me, cache, rows, queries, goal, docs.reshape(1, tok), docs.reshape(tok, 1))


def row_terms(w_k, w_v, dcache, feats):
    sections, _, _, part = w_k.shape
    tok = dcache.shape[0]
    width = w_k.size // part
    return pl.pallas_call(
        rows_kernel,
        out_shape=jax.ShapeDtypeStruct((sections, tok // sections * (width // feats), feats), BF16),
        in_specs=[whole()] * 3,
        out_specs=whole(),
        compiler_params=pltpu.CompilerParams(vmem_limit_bytes=8 * 2**20),
        cost_estimate=pl.CostEstimate(
            flops=4 * tok * width * part, bytes_accessed=4 * 2**20, transcendentals=0
        ),
        name="row_terms",
    )(w_k, w_v, dcache)


def add_kernel(*refs):
    total = refs[0][0].astype(F32)
    for ref in refs[1:-1]:
        total = total + ref[0].astype(F32)
    refs[-1][...] = total.astype(refs[-1].dtype).reshape(refs[-1].shape)


def add_term(*parts, flops=0, dtype=BF16):
    shape = parts[0][0].shape[1:]

    def spec(at):
        return pl.BlockSpec((1,) + shape, lambda i: (at,) + (0,) * len(shape))

    return pl.pallas_call(
        add_kernel,
        grid=(1,),
        out_shape=jax.ShapeDtypeStruct((1,) + shape, dtype),
        in_specs=[spec(at) for _, at in parts],
        out_specs=spec(0),
        compiler_params=pltpu.CompilerParams(vmem_limit_bytes=8 * 2**20),
        cost_estimate=pl.CostEstimate(flops=flops, bytes_accessed=2**20, transcendentals=0),
        name="add_term",
    )(*[array for array, _ in parts])


def reduce_groups(n):
    return [(0, 2, 6), (1, 3), (7, 5), (4,)] if n == 8 else [(0,), (1,)]


def reduce_scatter(parts, axis):
    n = lax.axis_size(axis)

    def send(x, places):
        return lax.ppermute(x, axis, [(i, (i + places) % n) for i in range(n)])

    if n == 2:
        return add_term((parts[0], 0), (send(parts[1], 1), 0))
    kept, up, down, far = parts
    up, down = send(up, 1), send(down, -1)
    up_two, down_two = add_term((kept, 1), (up, 1)), add_term((kept, 2), (down, 1))
    up_two, down_two, far = lax.optimization_barrier((up_two, down_two, far))
    up_two, down_two, far = send(up_two, 2), send(down_two, -2), send(far, 4)
    base = add_term((kept, 0), (up, 0), (down, 0), (far, 0), dtype=F32)
    return add_term((base, 0), (up_two, 0), (down_two, 0), flops=HOP_FLOPS)


def per_device(aux_rows, predictors, queries, target, lengths):
    sections = lax.axis_size("section")
    auxes = lax.axis_size("aux")
    shards = lax.axis_size("dp")
    both = ("section", "aux")
    peers = sections * auxes
    blk, width = predictors.shape[4:]
    part = width // auxes
    rows_each, feats = aux_rows.shape[2:]
    tok = sections * rows_each

    w_out = predictors.reshape(sections, blk, auxes, part).swapaxes(1, 2).reshape(peers, blk, part)
    w_out = (w_out * W_SCALE).astype(jnp.float16)
    w_in = lax.all_to_all(w_out, both, split_axis=0, concat_axis=0, tiled=True)

    r_out = double(aux_rows.reshape(sections, rows_each, feats), auxes).reshape(
        peers, rows_each, feats
    )
    w_in, r_out = lax.optimization_barrier((w_in, r_out))
    r_in = lax.all_to_all(r_out, both, split_axis=0, concat_axis=0, tiled=True)
    r_in = r_in.reshape(sections, auxes * rows_each, feats)

    w_all = lax.all_gather(w_in, "dp", axis=0)
    w_all = (w_all.astype(F32) * (1.0 / W_SCALE)).astype(BF16)
    w_all = w_all.reshape(shards, sections, auxes * blk, part)

    ends = jnp.cumsum(lengths[0])
    pos = jnp.arange(tok, dtype=jnp.int32)
    docs = jnp.sum((pos[:, None] >= ends[None, :]).astype(jnp.int32), axis=1)
    me = lax.axis_index("dp").astype(jnp.int32).reshape(1)
    cache, rows, w_k, w_v = project(w_all, r_in)
    *dw, dcache = attend(
        me, cache, rows, queries[0], target[0], docs, reduce_groups(shards), w_all.shape[1:]
    )

    r_send = row_terms(w_k, w_v, dcache, feats).reshape(peers, rows_each, feats)
    r_back = lax.all_to_all(r_send, both, split_axis=0, concat_axis=0, tiled=True)
    w_sum = reduce_scatter(dw, "dp")
    w_sum, r_back = lax.optimization_barrier((w_sum, r_back))
    w_back = lax.all_to_all(w_sum.reshape(peers, blk, part), both, split_axis=0, concat_axis=0, tiled=True)
    grad_predictors = (
        w_back.reshape(sections, auxes, blk, part).swapaxes(1, 2).reshape(predictors.shape)
    ).astype(F32)
    r_sum = jnp.sum(r_back.reshape(sections, auxes, rows_each, feats).astype(F32), axis=1)
    grad_rows = r_sum.astype(BF16).reshape(aux_rows.shape)
    return (grad_rows, grad_predictors)


def solution(mesh):
    return jax.shard_map(
        per_device,
        mesh=mesh,
        in_specs=(
            P(None, "dp", "section", "aux"),
            P("aux", None, "section", "dp", None, None),
            P("section", "dp", "aux"),
            P("section", "dp", "aux"),
            P("dp", None),
        ),
        out_specs=(P(None, "dp", "section", "aux"), P("aux", None, "section", "dp", None, None)),
        check_vma=False,
    )
```

```python
import functools
import math

import jax
import jax.numpy as jnp
from jax import lax
from jax.experimental import pallas as pl
from jax.experimental.pallas import tpu as pltpu
from jax.sharding import PartitionSpec as P

HEAD_DIM = 128
F32 = jnp.float32
BF16 = jnp.bfloat16
W_SCALE = 2.0**18
HOP_FLOPS = 16 * 10**9


def dot(a, b, dims):
    return lax.dot_general(a, b, (dims, ((), ())), preferred_element_type=F32)


NN = ((1,), (0,))
NT = ((1,), (1,))
TN = ((0,), (0,))


def order_weights(w_ref, wk_ref, wv_ref):
    shards, sections, two_blk, part = w_ref.shape
    blk = two_blk // 2
    for pair in range(shards // 2):
        one = w_ref[2 * pair].astype(F32)
        two = w_ref[2 * pair + 1].astype(F32)
        keys = jnp.concatenate([one[:, :blk], two[:, :blk]], axis=1)
        values = jnp.concatenate([one[:, blk:], two[:, blk:]], axis=1)
        wk_ref[:, pair] = keys.astype(BF16)
        wv_ref[:, pair] = values.astype(BF16)


def project_kernel(w_ref, r_ref, cache_ref, rows_ref, wk_ref, wv_ref):
    shards, sections, two_blk, part = w_ref.shape
    width = sections * shards * two_blk // 2
    tok = rows_ref.shape[0]
    feats = r_ref.shape[2]
    each = tok // sections

    order_weights(w_ref, wk_ref, wv_ref)
    pieces = r_ref[...].astype(F32)
    for a in range(width // feats):
        piece = pieces[:, a * each:(a + 1) * each, :]
        rows_ref[:, a * feats:(a + 1) * feats] = piece.reshape(tok, feats).astype(BF16)
    rows = rows_ref[...]
    cache_ref[:, :part] = dot(rows, wk_ref[...].reshape(width, part), NN).astype(BF16)
    cache_ref[:, part:] = dot(rows, wv_ref[...].reshape(width, part), NN).astype(BF16)


def attend_kernel(
    groups, me_ref, cache_ref, rows_ref, wk_ref, wv_ref, q_ref, g_ref, docr_ref, docc_ref, *refs
):
    part_refs, (out_any, dc_ref, bias_ref, dw_ref, out_ref, sem) = refs[:-6], refs[-6:]
    shards, sections, two_blk, part = dw_ref.shape
    blk = two_blk // 2
    tok = q_ref.shape[0]
    half = tok // 2
    keys = cache_ref[:, :part]
    values = cache_ref[:, part:]

    j_at = lax.broadcasted_iota(jnp.int32, (tok, tok), 0)
    i_at = lax.broadcasted_iota(jnp.int32, (tok, tok), 1)
    seen = (docc_ref[...] == docr_ref[...]) & (j_at <= i_at)
    bias_ref[...] = jnp.where(seen, 0.0, -1e30).astype(F32)

    scale = 1.0 / math.sqrt(HEAD_DIM)
    to_two = scale * math.log2(math.e)
    kv_heads = part // HEAD_DIM
    group = q_ref.shape[1] // part

    def softmax(s, bias):
        t = s * to_two + bias
        e = jnp.exp2(t - jnp.max(t, axis=0, keepdims=True))
        return e * (1.0 / jnp.sum(e, axis=0, keepdims=True))

    def whole_square(x_a, x_b):
        low = jnp.concatenate([x_a, jnp.zeros((half, half), BF16)], axis=0)
        return jnp.concatenate([low, x_b], axis=1)

    for h in range(kv_heads):
        k_h = keys[:, h * HEAD_DIM:(h + 1) * HEAD_DIM]
        v_h = values[:, h * HEAD_DIM:(h + 1) * HEAD_DIM]
        v_t = v_h.astype(F32).T.astype(BF16)

        def heads_of(h, k_h, v_h, v_t):
            at = [h * group + n for n in range(group)]
            cols = [pl.ds(pl.multiple_of(n * HEAD_DIM, HEAD_DIM), HEAD_DIM) for n in at]
            q = [q_ref[:, c] for c in cols]
            s = [dot(k_h, x, NT) for x in q]
            goal = [g_ref[:, c].T.astype(F32) for c in cols]
            p_a = [softmax(x[:half, :half], bias_ref[:half, :half]) for x in s]
            p_b = [softmax(x[:, half:], bias_ref[:, half:]) for x in s]
            p = [whole_square(x.astype(BF16), y.astype(BF16)) for x, y in zip(p_a, p_b)]
            out = [dot(v_t, x, NN) for x in p]
            dout = [x - y for x, y in zip(out, goal)]
            dout_b = [x.astype(BF16) for x in dout]
            dp = [dot(v_h, x, NN) for x in dout_b]
            delta = [jnp.sum(x * y, axis=0, keepdims=True) for x, y in zip(dout, out)]
            ds_a = [
                (x * (y[:half, :half] - z[:, :half]) * scale).astype(BF16)
                for x, y, z in zip(p_a, dp, delta)
            ]
            ds_b = [
                (x * (y[:, half:] - z[:, half:]) * scale).astype(BF16)
                for x, y, z in zip(p_b, dp, delta)
            ]
            ds = [whole_square(x, y) for x, y in zip(ds_a, ds_b)]
            dv = sum(dot(x, y, NT) for x, y in zip(p, dout_b))
            dk = sum(dot(x, y, NN) for x, y in zip(ds, q))
            return dk, dv

        dk, dv = heads_of(h, k_h, v_h, v_t)
        dc_ref[:, h * HEAD_DIM:(h + 1) * HEAD_DIM] = dk.astype(BF16)
        dc_ref[:, part + h * HEAD_DIM:part + (h + 1) * HEAD_DIM] = dv.astype(BF16)

    dcache = dc_ref[...]
    width = rows_ref.shape[1]
    feats = out_ref.shape[2]
    each = tok // sections
    w_k = wk_ref[...].reshape(width, part)
    w_v = wv_ref[...].reshape(width, part)
    terms = []
    for a in range(width // feats):
        span = slice(a * feats, (a + 1) * feats)
        term = dot(dcache[:, :part], w_k[span], NT) + dot(dcache[:, part:], w_v[span], NT)
        terms.append(term.reshape(sections, each, feats))
    out_ref[...] = jnp.concatenate(terms, axis=1).astype(BF16)
    out_copy = pltpu.make_async_copy(out_ref, out_any, sem)
    out_copy.start()

    me = me_ref[0]
    step_rows = 4 * shards * blk
    for at in range(sections // 4):
        x = rows_ref[:, at * step_rows:(at + 1) * step_rows]
        full = dot(x, dcache, TN).reshape(4, shards, blk, 2 * part)
        for d in range(shards):
            both = jnp.concatenate([full[:, d, :, :part], full[:, d, :, part:]], axis=1)
            dw_ref[lax.rem(d + shards - me, shards), at * 4:(at + 1) * 4] = both.astype(BF16)
    for group_at, ref in zip(groups, part_refs):
        for slot, k in enumerate(group_at):
            ref[slot] = dw_ref[k]
    out_copy.wait()


def double_kernel(x_ref, out_ref):
    for a in range(out_ref.shape[1]):
        out_ref[:, a] = x_ref[...]


def double(x, auxes):
    return pl.pallas_call(
        double_kernel,
        out_shape=jax.ShapeDtypeStruct((x.shape[0], auxes) + x.shape[1:], x.dtype),
        in_specs=[whole()],
        out_specs=whole(),
        compiler_params=pltpu.CompilerParams(vmem_limit_bytes=8 * 2**20),
        cost_estimate=pl.CostEstimate(flops=0, bytes_accessed=2 * (1 + auxes) * x.size, transcendentals=0),
        name="double",
    )(x)


def whole(space=pltpu.VMEM):
    return pl.BlockSpec(memory_space=space)


def project(w_all, r_in):
    shards, sections, two_blk, part = w_all.shape
    width = sections * shards * two_blk // 2
    tok = r_in.size // width
    ordered = jax.ShapeDtypeStruct((sections, shards // 2, two_blk, part), BF16)
    return pl.pallas_call(
        project_kernel,
        out_shape=(
            jax.ShapeDtypeStruct((tok, 2 * part), BF16),
            jax.ShapeDtypeStruct((tok, width), BF16),
            ordered,
            ordered,
        ),
        in_specs=[whole()] * 2,
        out_specs=(whole(),) * 4,
        compiler_params=pltpu.CompilerParams(vmem_limit_bytes=12 * 2**20),
        cost_estimate=pl.CostEstimate(
            flops=4 * tok * width * part, bytes_accessed=6 * 2**20, transcendentals=0
        ),
        name="project",
    )(w_all, r_in)


def attend(me, cache, rows, w_k, w_v, queries, goal, docs, groups, term, r_shape):
    tok = queries.shape[0]
    return pl.pallas_call(
        functools.partial(attend_kernel, groups),
        out_shape=tuple(jax.ShapeDtypeStruct((len(group),) + term, BF16) for group in groups)
        + (jax.ShapeDtypeStruct(r_shape, BF16),),
        in_specs=[whole(pltpu.SMEM)] + [whole()] * 8,
        out_specs=(whole(),) * len(groups) + (whole(pltpu.HBM),),
        scratch_shapes=[
            pltpu.VMEM(cache.shape, BF16),
            pltpu.VMEM((tok, tok), F32),
            pltpu.VMEM((sum(len(group) for group in groups),) + term, BF16),
            pltpu.VMEM(r_shape, BF16),
            pltpu.SemaphoreType.DMA,
        ],
        compiler_params=pltpu.CompilerParams(vmem_limit_bytes=18 * 2**20),
        cost_estimate=pl.CostEstimate(
            flops=2 * (2 * rows.size * cache.shape[1] + 5 * tok * queries.size),
            bytes_accessed=6 * 2**20,
            transcendentals=tok * queries.size // HEAD_DIM,
        ),
        name="attend",
    )(me, cache, rows, w_k, w_v, queries, goal, docs.reshape(1, tok), docs.reshape(tok, 1))


def add_kernel(*refs):
    total = refs[0][0].astype(F32)
    for ref in refs[1:-1]:
        total = total + ref[0].astype(F32)
    refs[-1][...] = total.astype(refs[-1].dtype).reshape(refs[-1].shape)


def add_term(*parts, flops=0, dtype=BF16):
    shape = parts[0][0].shape[1:]

    def spec(at):
        return pl.BlockSpec((1,) + shape, lambda i: (at,) + (0,) * len(shape))

    return pl.pallas_call(
        add_kernel,
        grid=(1,),
        out_shape=jax.ShapeDtypeStruct((1,) + shape, dtype),
        in_specs=[spec(at) for _, at in parts],
        out_specs=spec(0),
        compiler_params=pltpu.CompilerParams(vmem_limit_bytes=8 * 2**20),
        cost_estimate=pl.CostEstimate(flops=flops, bytes_accessed=2**20, transcendentals=0),
        name="add_term",
    )(*[array for array, _ in parts])


def reduce_groups(n):
    return [(0, 2, 6), (1, 3), (7, 5), (4,)] if n == 8 else [(0,), (1,)]


def reduce_scatter(parts, axis):
    n = lax.axis_size(axis)

    def send(x, places):
        return lax.ppermute(x, axis, [(i, (i + places) % n) for i in range(n)])

    if n == 2:
        return add_term((parts[0], 0), (send(parts[1], 1), 0))
    kept, up, down, far = parts
    up, down = send(up, 1), send(down, -1)
    up_two, down_two = add_term((kept, 1), (up, 1)), add_term((kept, 2), (down, 1))
    up_two, down_two, far = lax.optimization_barrier((up_two, down_two, far))
    up_two, down_two, far = send(up_two, 2), send(down_two, -2), send(far, 4)
    base = add_term((kept, 0), (up, 0), (down, 0), (far, 0), dtype=F32)
    return add_term((base, 0), (up_two, 0), (down_two, 0), flops=HOP_FLOPS)


def per_device(aux_rows, predictors, queries, target, lengths):
    sections = lax.axis_size("section")
    auxes = lax.axis_size("aux")
    shards = lax.axis_size("dp")
    both = ("section", "aux")
    peers = sections * auxes
    blk, width = predictors.shape[4:]
    part = width // auxes
    rows_each, feats = aux_rows.shape[2:]
    tok = sections * rows_each

    w_out = predictors.reshape(sections, blk, auxes, part).swapaxes(1, 2).reshape(peers, blk, part)
    w_out = (w_out * W_SCALE).astype(jnp.float16)
    w_in = lax.all_to_all(w_out, both, split_axis=0, concat_axis=0, tiled=True)

    r_out = double(aux_rows.reshape(sections, rows_each, feats), auxes).reshape(
        peers, rows_each, feats
    )
    w_in, r_out = lax.optimization_barrier((w_in, r_out))
    r_in = lax.all_to_all(r_out, both, split_axis=0, concat_axis=0, tiled=True)
    r_in = r_in.reshape(sections, auxes * rows_each, feats)

    w_all = lax.all_gather(w_in, "dp", axis=0)
    w_all = (w_all.astype(F32) * (1.0 / W_SCALE)).astype(BF16)
    w_all = w_all.reshape(shards, sections, auxes * blk, part)

    ends = jnp.cumsum(lengths[0])
    pos = jnp.arange(tok, dtype=jnp.int32)
    docs = jnp.sum((pos[:, None] >= ends[None, :]).astype(jnp.int32), axis=1)
    me = lax.axis_index("dp").astype(jnp.int32).reshape(1)
    cache, rows, w_k, w_v = project(w_all, r_in)
    *dw, r_send = attend(
        me, cache, rows, w_k, w_v, queries[0], target[0], docs,
        reduce_groups(shards), w_all.shape[1:], r_in.shape,
    )

    r_send = r_send.reshape(peers, rows_each, feats)
    r_back = lax.all_to_all(r_send, both, split_axis=0, concat_axis=0, tiled=True)
    w_sum = reduce_scatter(dw, "dp")
    w_sum, r_back = lax.optimization_barrier((w_sum, r_back))
    w_back = lax.all_to_all(w_sum.reshape(peers, blk, part), both, split_axis=0, concat_axis=0, tiled=True)
    grad_predictors = (
        w_back.reshape(sections, auxes, blk, part).swapaxes(1, 2).reshape(predictors.shape)
    ).astype(F32)
    r_sum = jnp.sum(r_back.reshape(sections, auxes, rows_each, feats).astype(F32), axis=1)
    grad_rows = r_sum.astype(BF16).reshape(aux_rows.shape)
    return (grad_rows, grad_predictors)


def solution(mesh):
    return jax.shard_map(
        per_device,
        mesh=mesh,
        in_specs=(
            P(None, "dp", "section", "aux"),
            P("aux", None, "section", "dp", None, None),
            P("section", "dp", "aux"),
            P("section", "dp", "aux"),
            P("dp", None),
        ),
        out_specs=(P(None, "dp", "section", "aux"), P("aux", None, "section", "dp", None, None)),
        check_vma=False,
    )
```

```python
import functools
import math

import jax
import jax.numpy as jnp
from jax import lax
from jax.experimental import pallas as pl
from jax.experimental.pallas import tpu as pltpu
from jax.sharding import PartitionSpec as P

HEAD_DIM = 128
F32 = jnp.float32
BF16 = jnp.bfloat16
W_SCALE = 2.0**18
HOP_FLOPS = 16 * 10**9


def dot(a, b, dims):
    return lax.dot_general(a, b, (dims, ((), ())), preferred_element_type=F32)


NN = ((1,), (0,))
NT = ((1,), (1,))


def order_weights(w_ref, wk_ref, wv_ref):
    shards, sections, two_blk, part = w_ref.shape
    blk = two_blk // 2
    for pair in range(shards // 2):
        one = w_ref[2 * pair].astype(F32)
        two = w_ref[2 * pair + 1].astype(F32)
        keys = jnp.concatenate([one[:, :blk], two[:, :blk]], axis=1)
        values = jnp.concatenate([one[:, blk:], two[:, blk:]], axis=1)
        wk_ref[:, pair] = keys.astype(BF16)
        wv_ref[:, pair] = values.astype(BF16)


def project_kernel(
    w_ref, r_ref, docr_ref, docc_ref, cache_ref, rowst_ref, wk_ref, wv_ref, bias_ref, rows_ref
):
    shards, sections, two_blk, part = w_ref.shape
    width = sections * shards * two_blk // 2
    tok = rows_ref.shape[0]
    feats = r_ref.shape[2]
    each = tok // sections

    order_weights(w_ref, wk_ref, wv_ref)
    pieces = r_ref[...].astype(F32)
    for a in range(width // feats):
        piece = pieces[:, a * each:(a + 1) * each, :]
        rows_ref[:, a * feats:(a + 1) * feats] = piece.reshape(tok, feats).astype(BF16)
    rows = rows_ref[...]
    cache_ref[:, :part] = dot(rows, wk_ref[...].reshape(width, part), NN).astype(BF16)
    cache_ref[:, part:] = dot(rows, wv_ref[...].reshape(width, part), NN).astype(BF16)
    rowst_ref[...] = rows.T

    j_at = lax.broadcasted_iota(jnp.int32, (tok, tok), 0)
    i_at = lax.broadcasted_iota(jnp.int32, (tok, tok), 1)
    seen = (docc_ref[...] == docr_ref[...]) & (j_at <= i_at)
    bias_ref[...] = jnp.where(seen, 0.0, -1e30).astype(F32)


def attend_kernel(
    groups, me_ref, cache_ref, rowst_ref, wk_ref, wv_ref, bias_ref, q_ref, g_ref, *refs
):
    part_refs, (out_any, dc_ref, dw_ref, out_ref, sem) = refs[:-5], refs[-5:]
    shards, sections, two_blk, part = dw_ref.shape
    blk = two_blk // 2
    tok = q_ref.shape[0]
    half = tok // 2
    keys = cache_ref[:, :part]
    values = cache_ref[:, part:]

    scale = 1.0 / math.sqrt(HEAD_DIM)
    to_two = scale * math.log2(math.e)
    kv_heads = part // HEAD_DIM
    group = q_ref.shape[1] // part

    def softmax(s, bias):
        t = s * to_two + bias
        e = jnp.exp2(t - jnp.max(t, axis=0, keepdims=True))
        return e * (1.0 / jnp.sum(e, axis=0, keepdims=True))

    def whole_square(x_a, x_b):
        low = jnp.concatenate([x_a, jnp.zeros((half, half), BF16)], axis=0)
        return jnp.concatenate([low, x_b], axis=1)

    for h in range(kv_heads):
        k_h = keys[:, h * HEAD_DIM:(h + 1) * HEAD_DIM]
        v_h = values[:, h * HEAD_DIM:(h + 1) * HEAD_DIM]
        v_t = v_h.astype(F32).T.astype(BF16)

        def heads_of(h, k_h, v_h, v_t):
            at = [h * group + n for n in range(group)]
            cols = [pl.ds(pl.multiple_of(n * HEAD_DIM, HEAD_DIM), HEAD_DIM) for n in at]
            q = [q_ref[:, c] for c in cols]
            s = [dot(k_h, x, NT) for x in q]
            goal = [g_ref[:, c].T.astype(F32) for c in cols]
            p_a = [softmax(x[:half, :half], bias_ref[:half, :half]) for x in s]
            p_b = [softmax(x[:, half:], bias_ref[:, half:]) for x in s]
            p = [whole_square(x.astype(BF16), y.astype(BF16)) for x, y in zip(p_a, p_b)]
            out = [dot(v_t, x, NN) for x in p]
            dout = [x - y for x, y in zip(out, goal)]
            dout_b = [x.astype(BF16) for x in dout]
            dp = [dot(v_h, x, NN) for x in dout_b]
            delta = [jnp.sum(x * y, axis=0, keepdims=True) for x, y in zip(dout, out)]
            ds_a = [
                (x * (y[:half, :half] - z[:, :half]) * scale).astype(BF16)
                for x, y, z in zip(p_a, dp, delta)
            ]
            ds_b = [
                (x * (y[:, half:] - z[:, half:]) * scale).astype(BF16)
                for x, y, z in zip(p_b, dp, delta)
            ]
            ds = [whole_square(x, y) for x, y in zip(ds_a, ds_b)]
            dv = sum(dot(x, y, NT) for x, y in zip(p, dout_b))
            dk = sum(dot(x, y, NN) for x, y in zip(ds, q))
            return dk, dv

        dk, dv = heads_of(h, k_h, v_h, v_t)
        dc_ref[:, h * HEAD_DIM:(h + 1) * HEAD_DIM] = dk.astype(BF16)
        dc_ref[:, part + h * HEAD_DIM:part + (h + 1) * HEAD_DIM] = dv.astype(BF16)

    dcache = dc_ref[...]
    width = rowst_ref.shape[0]
    feats = out_ref.shape[2]
    each = tok // sections
    w_k = wk_ref[...].reshape(width, part)
    w_v = wv_ref[...].reshape(width, part)
    terms = []
    for a in range(width // feats):
        span = slice(a * feats, (a + 1) * feats)
        term = dot(dcache[:, :part], w_k[span], NT) + dot(dcache[:, part:], w_v[span], NT)
        terms.append(term.reshape(sections, each, feats))
    out_ref[...] = jnp.concatenate(terms, axis=1).astype(BF16)
    out_copy = pltpu.make_async_copy(out_ref, out_any, sem)
    out_copy.start()

    me = me_ref[0]
    step_rows = 4 * shards * blk
    for at in range(sections // 4):
        x = rowst_ref[at * step_rows:(at + 1) * step_rows, :]
        full = dot(x, dcache, NN).reshape(4, shards, blk, 2 * part)
        for d in range(shards):
            both = jnp.concatenate([full[:, d, :, :part], full[:, d, :, part:]], axis=1)
            dw_ref[lax.rem(d + shards - me, shards), at * 4:(at + 1) * 4] = both.astype(BF16)
    for group_at, ref in zip(groups, part_refs):
        for slot, k in enumerate(group_at):
            ref[slot] = dw_ref[k]
    out_copy.wait()


def double_kernel(x_ref, out_ref):
    for a in range(out_ref.shape[1]):
        out_ref[:, a] = x_ref[...]


def double(x, auxes):
    return pl.pallas_call(
        double_kernel,
        out_shape=jax.ShapeDtypeStruct((x.shape[0], auxes) + x.shape[1:], x.dtype),
        in_specs=[whole()],
        out_specs=whole(),
        compiler_params=pltpu.CompilerParams(vmem_limit_bytes=8 * 2**20),
        cost_estimate=pl.CostEstimate(flops=0, bytes_accessed=2 * (1 + auxes) * x.size, transcendentals=0),
        name="double",
    )(x)


def whole(space=pltpu.VMEM):
    return pl.BlockSpec(memory_space=space)


def project(w_all, r_in, docs):
    shards, sections, two_blk, part = w_all.shape
    width = sections * shards * two_blk // 2
    tok = r_in.size // width
    ordered = jax.ShapeDtypeStruct((sections, shards // 2, two_blk, part), BF16)
    return pl.pallas_call(
        project_kernel,
        out_shape=(
            jax.ShapeDtypeStruct((tok, 2 * part), BF16),
            jax.ShapeDtypeStruct((width, tok), BF16),
            ordered,
            ordered,
            jax.ShapeDtypeStruct((tok, tok), F32),
        ),
        in_specs=[whole()] * 4,
        out_specs=(whole(),) * 5,
        scratch_shapes=[pltpu.VMEM((tok, width), BF16)],
        compiler_params=pltpu.CompilerParams(vmem_limit_bytes=12 * 2**20),
        cost_estimate=pl.CostEstimate(
            flops=4 * tok * width * part, bytes_accessed=6 * 2**20, transcendentals=0
        ),
        name="project",
    )(w_all, r_in, docs.reshape(1, tok), docs.reshape(tok, 1))


def attend(me, cache, rows_t, w_k, w_v, bias, queries, goal, groups, term, r_shape):
    tok = queries.shape[0]
    return pl.pallas_call(
        functools.partial(attend_kernel, groups),
        out_shape=tuple(jax.ShapeDtypeStruct((len(group),) + term, BF16) for group in groups)
        + (jax.ShapeDtypeStruct(r_shape, BF16),),
        in_specs=[whole(pltpu.SMEM)] + [whole()] * 7,
        out_specs=(whole(),) * len(groups) + (whole(pltpu.HBM),),
        scratch_shapes=[
            pltpu.VMEM(cache.shape, BF16),
            pltpu.VMEM((sum(len(group) for group in groups),) + term, BF16),
            pltpu.VMEM(r_shape, BF16),
            pltpu.SemaphoreType.DMA,
        ],
        compiler_params=pltpu.CompilerParams(vmem_limit_bytes=18 * 2**20),
        cost_estimate=pl.CostEstimate(
            flops=2 * (2 * rows_t.size * cache.shape[1] + 5 * tok * queries.size),
            bytes_accessed=6 * 2**20,
            transcendentals=tok * queries.size // HEAD_DIM,
        ),
        name="attend",
    )(me, cache, rows_t, w_k, w_v, bias, queries, goal)


def add_kernel(*refs):
    total = refs[0][0].astype(F32)
    for ref in refs[1:-1]:
        total = total + ref[0].astype(F32)
    refs[-1][...] = total.astype(refs[-1].dtype).reshape(refs[-1].shape)


def add_term(*parts, flops=0, dtype=BF16):
    shape = parts[0][0].shape[1:]

    def spec(at):
        return pl.BlockSpec((1,) + shape, lambda i: (at,) + (0,) * len(shape))

    return pl.pallas_call(
        add_kernel,
        grid=(1,),
        out_shape=jax.ShapeDtypeStruct((1,) + shape, dtype),
        in_specs=[spec(at) for _, at in parts],
        out_specs=spec(0),
        compiler_params=pltpu.CompilerParams(vmem_limit_bytes=8 * 2**20),
        cost_estimate=pl.CostEstimate(flops=flops, bytes_accessed=2**20, transcendentals=0),
        name="add_term",
    )(*[array for array, _ in parts])


def reduce_groups(n):
    return [(0, 2, 6), (1, 3), (7, 5), (4,)] if n == 8 else [(0,), (1,)]


def reduce_scatter(parts, axis):
    n = lax.axis_size(axis)

    def send(x, places):
        return lax.ppermute(x, axis, [(i, (i + places) % n) for i in range(n)])

    if n == 2:
        return add_term((parts[0], 0), (send(parts[1], 1), 0))
    kept, up, down, far = parts
    up, down = send(up, 1), send(down, -1)
    up_two, down_two = add_term((kept, 1), (up, 1)), add_term((kept, 2), (down, 1))
    down_two, far = lax.optimization_barrier((down_two, far))
    up_two, down_two, far = send(up_two, 2), send(down_two, -2), send(far, 4)
    base = add_term((kept, 0), (up, 0), (down, 0), (far, 0), dtype=F32)
    return add_term((base, 0), (up_two, 0), (down_two, 0), flops=HOP_FLOPS)


def per_device(aux_rows, predictors, queries, target, lengths):
    sections = lax.axis_size("section")
    auxes = lax.axis_size("aux")
    shards = lax.axis_size("dp")
    both = ("section", "aux")
    peers = sections * auxes
    blk, width = predictors.shape[4:]
    part = width // auxes
    rows_each, feats = aux_rows.shape[2:]
    tok = sections * rows_each

    w_out = predictors.reshape(sections, blk, auxes, part).swapaxes(1, 2).reshape(peers, blk, part)
    w_out = (w_out * W_SCALE).astype(jnp.float16)
    w_in = lax.all_to_all(w_out, both, split_axis=0, concat_axis=0, tiled=True)

    r_out = double(aux_rows.reshape(sections, rows_each, feats), auxes).reshape(
        peers, rows_each, feats
    )
    w_in, r_out = lax.optimization_barrier((w_in, r_out))
    r_in = lax.all_to_all(r_out, both, split_axis=0, concat_axis=0, tiled=True)
    r_in = r_in.reshape(sections, auxes * rows_each, feats)

    w_all = lax.all_gather(w_in, "dp", axis=0)
    w_all = (w_all.astype(F32) * (1.0 / W_SCALE)).astype(BF16)
    w_all = w_all.reshape(shards, sections, auxes * blk, part)

    ends = jnp.cumsum(lengths[0])
    pos = jnp.arange(tok, dtype=jnp.int32)
    docs = jnp.sum((pos[:, None] >= ends[None, :]).astype(jnp.int32), axis=1)
    me = lax.axis_index("dp").astype(jnp.int32).reshape(1)
    cache, rows_t, w_k, w_v, bias = project(w_all, r_in, docs)
    *dw, r_send = attend(
        me, cache, rows_t, w_k, w_v, bias, queries[0], target[0],
        reduce_groups(shards), w_all.shape[1:], r_in.shape,
    )

    r_send = r_send.reshape(peers, rows_each, feats)
    r_back = lax.all_to_all(r_send, both, split_axis=0, concat_axis=0, tiled=True)
    w_sum = reduce_scatter(dw, "dp")
    w_sum, r_back = lax.optimization_barrier((w_sum, r_back))
    w_back = lax.all_to_all(w_sum.reshape(peers, blk, part), both, split_axis=0, concat_axis=0, tiled=True)
    grad_predictors = (
        w_back.reshape(sections, auxes, blk, part).swapaxes(1, 2).reshape(predictors.shape)
    ).astype(F32)
    r_sum = jnp.sum(r_back.reshape(sections, auxes, rows_each, feats).astype(F32), axis=1)
    grad_rows = r_sum.astype(BF16).reshape(aux_rows.shape)
    return (grad_rows, grad_predictors)


def solution(mesh):
    return jax.shard_map(
        per_device,
        mesh=mesh,
        in_specs=(
            P(None, "dp", "section", "aux"),
            P("aux", None, "section", "dp", None, None),
            P("section", "dp", "aux"),
            P("section", "dp", "aux"),
            P("dp", None),
        ),
        out_specs=(P(None, "dp", "section", "aux"), P("aux", None, "section", "dp", None, None)),
        check_vma=False,
    )
```

```python
import functools
import math

import jax
import jax.numpy as jnp
from jax import lax
from jax.experimental import pallas as pl
from jax.experimental.pallas import tpu as pltpu
from jax.sharding import PartitionSpec as P

HEAD_DIM = 128
F32 = jnp.float32
BF16 = jnp.bfloat16
W_SCALE = 2.0**18
HOP_FLOPS = 17 * 10**9


def dot(a, b, dims):
    return lax.dot_general(a, b, (dims, ((), ())), preferred_element_type=F32)


NN = ((1,), (0,))
NT = ((1,), (1,))
TN = ((0,), (0,))


def order_weights(w_ref, wk_ref, wv_ref):
    shards, sections, two_blk, part = w_ref.shape
    blk = two_blk // 2
    for pair in range(shards // 2):
        one = w_ref[2 * pair].astype(F32)
        two = w_ref[2 * pair + 1].astype(F32)
        keys = jnp.concatenate([one[:, :blk], two[:, :blk]], axis=1)
        values = jnp.concatenate([one[:, blk:], two[:, blk:]], axis=1)
        wk_ref[:, pair] = keys.astype(BF16)
        wv_ref[:, pair] = values.astype(BF16)


def project_kernel(w_ref, r_ref, cache_ref, rows_ref, wk_ref, wv_ref):
    shards, sections, two_blk, part = w_ref.shape
    width = sections * shards * two_blk // 2
    tok = rows_ref.shape[0]
    feats = r_ref.shape[2]
    each = tok // sections

    order_weights(w_ref, wk_ref, wv_ref)
    pieces = r_ref[...].astype(F32)
    for a in range(width // feats):
        piece = pieces[:, a * each:(a + 1) * each, :]
        rows_ref[:, a * feats:(a + 1) * feats] = piece.reshape(tok, feats).astype(BF16)
    rows = rows_ref[...]
    cache_ref[:, :part] = dot(rows, wk_ref[...].reshape(width, part), NN).astype(BF16)
    cache_ref[:, part:] = dot(rows, wv_ref[...].reshape(width, part), NN).astype(BF16)


def attend_kernel(
    groups, me_ref, cache_ref, rows_ref, wk_ref, wv_ref, q_ref, g_ref, docr_ref, docc_ref, *refs
):
    part_refs, (out_any, dc_ref, bias_ref, dw_ref, out_ref, sem) = refs[:-6], refs[-6:]
    shards, sections, two_blk, part = dw_ref.shape
    blk = two_blk // 2
    tok = q_ref.shape[0]
    half = tok // 2
    keys = cache_ref[:, :part]
    values = cache_ref[:, part:]

    j_at = lax.broadcasted_iota(jnp.int32, (tok, tok), 0)
    i_at = lax.broadcasted_iota(jnp.int32, (tok, tok), 1)
    seen = (docc_ref[...] == docr_ref[...]) & (j_at <= i_at)
    bias_ref[...] = jnp.where(seen, 0.0, -1e30).astype(F32)

    scale = 1.0 / math.sqrt(HEAD_DIM)
    to_two = scale * math.log2(math.e)
    kv_heads = part // HEAD_DIM
    group = q_ref.shape[1] // part

    def softmax(s, bias):
        t = s * to_two + bias
        e = jnp.exp2(t - jnp.max(t, axis=0, keepdims=True))
        return e * (1.0 / jnp.sum(e, axis=0, keepdims=True))

    def whole_square(x_a, x_b):
        low = jnp.concatenate([x_a, jnp.zeros((half, half), BF16)], axis=0)
        return jnp.concatenate([low, x_b], axis=1)

    for h in range(kv_heads):
        k_h = keys[:, h * HEAD_DIM:(h + 1) * HEAD_DIM]
        v_h = values[:, h * HEAD_DIM:(h + 1) * HEAD_DIM]
        v_t = v_h.astype(F32).T.astype(BF16)

        def heads_of(h, k_h, v_h, v_t):
            at = [h * group + n for n in range(group)]
            cols = [pl.ds(pl.multiple_of(n * HEAD_DIM, HEAD_DIM), HEAD_DIM) for n in at]
            q = [q_ref[:, c] for c in cols]
            s = [dot(k_h, x, NT) for x in q]
            goal = [g_ref[:, c].T.astype(F32) for c in cols]
            p_a = [softmax(x[:half, :half], bias_ref[:half, :half]) for x in s]
            p_b = [softmax(x[:, half:], bias_ref[:, half:]) for x in s]
            p = [whole_square(x.astype(BF16), y.astype(BF16)) for x, y in zip(p_a, p_b)]
            out = [dot(v_t, x, NN) for x in p]
            dout = [x - y for x, y in zip(out, goal)]
            dout_b = [x.astype(BF16) for x in dout]
            dp = [dot(v_h, x, NN) for x in dout_b]
            delta = [jnp.sum(x * y, axis=0, keepdims=True) for x, y in zip(dout, out)]
            ds_a = [
                (x * (y[:half, :half] - z[:, :half]) * scale).astype(BF16)
                for x, y, z in zip(p_a, dp, delta)
            ]
            ds_b = [
                (x * (y[:, half:] - z[:, half:]) * scale).astype(BF16)
                for x, y, z in zip(p_b, dp, delta)
            ]
            ds = [whole_square(x, y) for x, y in zip(ds_a, ds_b)]
            dv = sum(dot(x, y, NT) for x, y in zip(p, dout_b))
            dk = sum(dot(x, y, NN) for x, y in zip(ds, q))
            return dk, dv

        dk, dv = heads_of(h, k_h, v_h, v_t)
        dc_ref[:, h * HEAD_DIM:(h + 1) * HEAD_DIM] = dk.astype(BF16)
        dc_ref[:, part + h * HEAD_DIM:part + (h + 1) * HEAD_DIM] = dv.astype(BF16)

    dcache = dc_ref[...]
    width = rows_ref.shape[1]
    feats = out_ref.shape[2]
    each = tok // sections
    w_k = wk_ref[...].reshape(width, part)
    w_v = wv_ref[...].reshape(width, part)
    terms = []
    for a in range(width // feats):
        span = slice(a * feats, (a + 1) * feats)
        term = dot(dcache[:, :part], w_k[span], NT) + dot(dcache[:, part:], w_v[span], NT)
        terms.append(term.reshape(sections, each, feats))
    out_ref[...] = jnp.concatenate(terms, axis=1).astype(BF16)
    out_copy = pltpu.make_async_copy(out_ref, out_any, sem)
    out_copy.start()

    me = me_ref[0]
    step_rows = 4 * shards * blk
    for at in range(sections // 4):
        x = rows_ref[:, at * step_rows:(at + 1) * step_rows]
        full = dot(x, dcache, TN).reshape(4, shards, blk, 2 * part)
        for d in range(shards):
            both = jnp.concatenate([full[:, d, :, :part], full[:, d, :, part:]], axis=1)
            dw_ref[lax.rem(d + shards - me, shards), at * 4:(at + 1) * 4] = both.astype(BF16)
    for group_at, ref in zip(groups, part_refs):
        for slot, k in enumerate(group_at):
            ref[slot] = dw_ref[k]
    out_copy.wait()


def double_kernel(x_ref, out_ref):
    for a in range(out_ref.shape[1]):
        out_ref[:, a] = x_ref[...]


def double(x, auxes):
    return pl.pallas_call(
        double_kernel,
        out_shape=jax.ShapeDtypeStruct((x.shape[0], auxes) + x.shape[1:], x.dtype),
        in_specs=[whole()],
        out_specs=whole(),
        compiler_params=pltpu.CompilerParams(vmem_limit_bytes=8 * 2**20),
        cost_estimate=pl.CostEstimate(flops=0, bytes_accessed=2 * (1 + auxes) * x.size, transcendentals=0),
        name="double",
    )(x)


def whole(space=pltpu.VMEM):
    return pl.BlockSpec(memory_space=space)


def project(w_all, r_in):
    shards, sections, two_blk, part = w_all.shape
    width = sections * shards * two_blk // 2
    tok = r_in.size // width
    ordered = jax.ShapeDtypeStruct((sections, shards // 2, two_blk, part), BF16)
    return pl.pallas_call(
        project_kernel,
        out_shape=(
            jax.ShapeDtypeStruct((tok, 2 * part), BF16),
            jax.ShapeDtypeStruct((tok, width), BF16),
            ordered,
            ordered,
        ),
        in_specs=[whole()] * 2,
        out_specs=(whole(),) * 4,
        compiler_params=pltpu.CompilerParams(vmem_limit_bytes=12 * 2**20),
        cost_estimate=pl.CostEstimate(
            flops=4 * tok * width * part, bytes_accessed=6 * 2**20, transcendentals=0
        ),
        name="project",
    )(w_all, r_in)


def attend(me, cache, rows, w_k, w_v, queries, goal, docs, groups, term, r_shape):
    tok = queries.shape[0]
    return pl.pallas_call(
        functools.partial(attend_kernel, groups),
        out_shape=tuple(jax.ShapeDtypeStruct((len(group),) + term, BF16) for group in groups)
        + (jax.ShapeDtypeStruct(r_shape, BF16),),
        in_specs=[whole(pltpu.SMEM)] + [whole()] * 8,
        out_specs=(whole(),) * len(groups) + (whole(pltpu.HBM),),
        scratch_shapes=[
            pltpu.VMEM(cache.shape, BF16),
            pltpu.VMEM((tok, tok), F32),
            pltpu.VMEM((sum(len(group) for group in groups),) + term, BF16),
            pltpu.VMEM(r_shape, BF16),
            pltpu.SemaphoreType.DMA,
        ],
        compiler_params=pltpu.CompilerParams(vmem_limit_bytes=18 * 2**20),
        cost_estimate=pl.CostEstimate(
            flops=2 * (2 * rows.size * cache.shape[1] + 5 * tok * queries.size),
            bytes_accessed=6 * 2**20,
            transcendentals=tok * queries.size // HEAD_DIM,
        ),
        name="attend",
    )(me, cache, rows, w_k, w_v, queries, goal, docs.reshape(1, tok), docs.reshape(tok, 1))


def add_kernel(*refs):
    total = refs[0][0].astype(F32)
    for ref in refs[1:-1]:
        total = total + ref[0].astype(F32)
    refs[-1][...] = total.astype(refs[-1].dtype).reshape(refs[-1].shape)


def add_term(*parts, flops=0, dtype=BF16):
    shape = parts[0][0].shape[1:]

    def spec(at):
        return pl.BlockSpec((1,) + shape, lambda i: (at,) + (0,) * len(shape))

    return pl.pallas_call(
        add_kernel,
        grid=(1,),
        out_shape=jax.ShapeDtypeStruct((1,) + shape, dtype),
        in_specs=[spec(at) for _, at in parts],
        out_specs=spec(0),
        compiler_params=pltpu.CompilerParams(vmem_limit_bytes=8 * 2**20),
        cost_estimate=pl.CostEstimate(flops=flops, bytes_accessed=2**20, transcendentals=0),
        name="add_term",
    )(*[array for array, _ in parts])


def reduce_groups(n):
    return [(0, 2, 6), (1, 3), (7, 5), (4,)] if n == 8 else [(0,), (1,)]


def reduce_scatter(parts, axis):
    n = lax.axis_size(axis)

    def send(x, places):
        return lax.ppermute(x, axis, [(i, (i + places) % n) for i in range(n)])

    if n == 2:
        return add_term((parts[0], 0), (send(parts[1], 1), 0))
    kept, up, down, far = parts
    up, down, far = lax.optimization_barrier((send(up, 1), send(down, -1), send(far, 4)))
    up_two = send(add_term((kept, 1), (up, 1)), 2)
    down_two = send(add_term((kept, 2), (down, 1)), -2)
    base = add_term((kept, 0), (up, 0), (down, 0), (far, 0), dtype=F32)
    return add_term((base, 0), (up_two, 0), (down_two, 0), flops=HOP_FLOPS)


def per_device(aux_rows, predictors, queries, target, lengths):
    sections = lax.axis_size("section")
    auxes = lax.axis_size("aux")
    shards = lax.axis_size("dp")
    both = ("section", "aux")
    peers = sections * auxes
    blk, width = predictors.shape[4:]
    part = width // auxes
    rows_each, feats = aux_rows.shape[2:]
    tok = sections * rows_each

    w_out = predictors.reshape(sections, blk, auxes, part).swapaxes(1, 2).reshape(peers, blk, part)
    w_out = (w_out * W_SCALE).astype(jnp.float16)
    w_in = lax.all_to_all(w_out, both, split_axis=0, concat_axis=0, tiled=True)

    r_out = double(aux_rows.reshape(sections, rows_each, feats), auxes).reshape(
        peers, rows_each, feats
    )
    w_in, r_out = lax.optimization_barrier((w_in, r_out))
    r_in = lax.all_to_all(r_out, both, split_axis=0, concat_axis=0, tiled=True)
    r_in = r_in.reshape(sections, auxes * rows_each, feats)

    w_all = lax.all_gather(w_in, "dp", axis=0)
    w_all = (w_all.astype(F32) * (1.0 / W_SCALE)).astype(BF16)
    w_all = w_all.reshape(shards, sections, auxes * blk, part)

    ends = jnp.cumsum(lengths[0])
    pos = jnp.arange(tok, dtype=jnp.int32)
    docs = jnp.sum((pos[:, None] >= ends[None, :]).astype(jnp.int32), axis=1)
    me = lax.axis_index("dp").astype(jnp.int32).reshape(1)
    cache, rows, w_k, w_v = project(w_all, r_in)
    *dw, r_send = attend(
        me, cache, rows, w_k, w_v, queries[0], target[0], docs,
        reduce_groups(shards), w_all.shape[1:], r_in.shape,
    )

    r_send = r_send.reshape(peers, rows_each, feats)
    r_back = lax.all_to_all(r_send, both, split_axis=0, concat_axis=0, tiled=True)
    w_sum = reduce_scatter(dw, "dp")
    w_sum, r_back = lax.optimization_barrier((w_sum, r_back))
    w_back = lax.all_to_all(w_sum.reshape(peers, blk, part), both, split_axis=0, concat_axis=0, tiled=True)
    grad_predictors = (
        w_back.reshape(sections, auxes, blk, part).swapaxes(1, 2).reshape(predictors.shape)
    ).astype(F32)
    r_sum = jnp.sum(r_back.reshape(sections, auxes, rows_each, feats).astype(F32), axis=1)
    grad_rows = r_sum.astype(BF16).reshape(aux_rows.shape)
    return (grad_rows, grad_predictors)


def solution(mesh):
    return jax.shard_map(
        per_device,
        mesh=mesh,
        in_specs=(
            P(None, "dp", "section", "aux"),
            P("aux", None, "section", "dp", None, None),
            P("section", "dp", "aux"),
            P("section", "dp", "aux"),
            P("dp", None),
        ),
        out_specs=(P(None, "dp", "section", "aux"), P("aux", None, "section", "dp", None, None)),
        check_vma=False,
    )
```
